32 devices in a mesh: groups: 2 (over x), wide: 16 (over z, y, core).
Axes of the slice: x: 2, y: 2, z: 4, core: 2. Of those that a mesh axis runs over, the one named last changes fastest.
Arguments:
- queries: bfloat16 [32, 12, 8192], P(('groups', 'wide')), parts along dimension 0, may hold values from -4.5 to 4.5
- prefix_kv: bfloat16 [32, 2, 1024, 1024], P(('groups', 'wide')), parts along dimension 0, may hold values from -4.5 to 4.5
- suffix_kv: bfloat16 [32, 12, 2, 64, 1024], P(('groups', 'wide')), parts along dimension 0, may hold values from -4.5 to 4.5
- counts: int32 [32], P('groups'), parts along dimension 0, may hold values from 1 to 12, 128 in all
- residual: bfloat16 [384, 8192], P('groups', 'wide'), parts along dimension 0, may hold values from -16 to 16
- out_weight: bfloat16 [8192, 8192], P(None, 'wide'), may hold values from -0.5 to 0.5
- norm_gain: float32 [8192], replicated, may hold values from 0.1 to 1.9
- qkv_weight: bfloat16 [8192, 10240], P(None, 'wide'), may hold values from -0.0625 to 0.0625
- owners: int32 [16, 8], replicated, may hold values from 0 to 15, as said below
Outputs:
- regrouped: bfloat16 [32, 2, 12, 8, 1280], P(('groups', 'wide')), parts along dimension 0
The draws below stay inside these ranges and needn't reach their ends.
There are 2 independent parts, one for each index of `groups`. The reference program is written for one: setup_inputs(seed, part) draws one part's arguments, and reference() takes and returns one part's arrays. A program takes and returns all parts, laid end to end along the dimension named above; an argument that names none is the same for every part. Nothing has to cross between parts.
Inputs may be any that keep to these rules, and one draw needn't show every extreme that they name: counts[p] rows of parent p are live, in slots 0 to counts[p] - 1; they sum to 128 and the largest is 12. `owners`: within each key-value group every device owns at most 2 parents; in every group some devices own exactly 2 and some none.
All inputs are finite; a program needn't handle non-finite values.
Results may differ from the reference program's by a relative error of at most 0.012.
Values may be sent and summed in bfloat16 or wider, within the bound.
A program may use at most 128 MiB of HBM per device.

```python
import math
import jax
import jax.numpy as jnp
import numpy as np
from jax import lax

KVH = 8
HD = 128
D = 8192
GQ = 8
GCOLS = 1280
QCOLS = 10240
CTX = 1024
SUF = 64
CAP = 12
OWN_G = 2
PARENTS = 16
ROWS = 128
SLOTS = 192
N_WIDE = 16


def draw_queries(key, part):
    noise_key = jax.random.fold_in(key, 1)
    shape_full = (PARENTS, CAP, KVH, GQ, HD)
    values = jnp.clip(1.5 * jax.random.normal(noise_key, shape_full, jnp.float32), -4.5, 4.5)
    return values.reshape(PARENTS, CAP, D).astype(jnp.bfloat16)


def draw_prefix_kv(key, part):
    noise_key = jax.random.fold_in(key, 2)
    shape_full = (PARENTS, 2, CTX, KVH, HD)
    values = jnp.clip(jax.random.normal(noise_key, shape_full, jnp.float32), -4.5, 4.5)
    return values.reshape(PARENTS, 2, CTX, KVH * HD).astype(jnp.bfloat16)


def draw_residual(key, part):
    sample_key = jax.random.fold_in(key, 5)
    column_key, row_key, noise_key = jax.random.split(sample_key, 3)
    columns = jnp.arange(D).astype(jnp.float32) / D
    column_scale = 3.0 ** columns * jnp.exp(jax.random.uniform(column_key, (D,), jnp.float32) * jnp.log(3.4)) / 2.2
    row_scale = jnp.exp(jax.random.uniform(row_key, (SLOTS, 1), jnp.float32) * jnp.log(10.0)) / 3.0
    values = jax.random.normal(noise_key, (SLOTS, D), jnp.float32)
    return jnp.clip(values * row_scale * column_scale, -16.0, 16.0).astype(jnp.bfloat16)


def draw_owners(key, part):
    quarter = PARENTS // 4
    owner_columns = []
    for kv_group in range(KVH):
        group_key = jax.random.fold_in(key, 17 + kv_group)
        device_key, order_key = jax.random.split(group_key)
        device_order = jax.random.permutation(device_key, PARENTS)
        slot_list = jnp.concatenate([jnp.repeat(device_order[:quarter], 2), device_order[2 * quarter:]])
        parent_order = jax.random.permutation(order_key, PARENTS)
        owner_columns.append(jnp.zeros((PARENTS,), jnp.int32).at[parent_order].set(slot_list.astype(jnp.int32)))
    return jnp.stack(owner_columns, axis=1).astype(jnp.int32)


def block_levels(key, extent, pieces, low, high):
    level, own = 1.0, jax.random.fold_in(key, 6)
    for dim, parts in pieces:
        draws = jnp.exp(jax.random.uniform(jax.random.fold_in(own, dim), (parts,), jnp.float32, low / len(pieces), high / len(pieces)))
        level = level * jnp.repeat(draws, extent[dim] // parts).reshape([-1 if axis == dim else 1 for axis in range(len(extent))])
    return level


def split_up(amount, total, most, lean):
    portions = [(1 << 20) // math.isqrt(standing ** lean) + 1 for standing in range(2, amount + 1)]
    surplus, given = total - most - (amount - 1), [1] * (amount - 1)
    while surplus > 0:
        candidates = [i for i in range(amount - 1) if given[i] < most]
        mass, budget = sum([portions[i] for i in candidates]), surplus
        for i in candidates:
            addition = min(most - given[i], max(1, budget * portions[i] // mass), surplus)
            given[i] = given[i] + addition
            surplus = surplus - addition
    return np.array([most] + given)


def uneven_parts(rng, amount, total, limit, skew):
    if amount == 2:
        one = jax.random.randint(rng, (), max(1, total - limit), min(limit, total - 1) + 1)
        return jnp.stack([one, total - one])
    sizes = jnp.asarray(split_up(amount, total, limit, skew), jnp.int32)
    twos = (amount - 1) // 2
    donor, receiver = sizes[1:1 + 2 * twos:2], sizes[2:2 + 2 * twos:2]
    slack = jnp.minimum(donor - 1, limit - receiver)
    passed = jax.random.randint(jax.random.fold_in(rng, 1), (twos,), 0, 1 << 20) % (slack + 1)
    sizes = sizes.at[1:1 + 2 * twos:2].set(donor - passed).at[2:2 + 2 * twos:2].set(receiver + passed)
    return sizes[jax.random.permutation(jax.random.fold_in(rng, 2), amount)]


def scatter_about(rng, dims, deviation, most, cuts=(), kind=jnp.bfloat16):
    loudness = block_levels(rng, dims, cuts, -0.22, 0.18) if cuts else 1.0
    result = jax.random.normal(rng, dims, jnp.float32) * deviation * loudness
    return jnp.minimum(jnp.maximum(result, -most), most).astype(kind)


def setup_inputs(seed: int = 0, part: int = 0) -> dict:
    splits = jax.random.split(jax.random.key(seed), 10)
    part_splits = jax.random.split(jax.random.fold_in(splits[9], part), 10)
    queries = draw_queries(jax.random.fold_in(jax.random.fold_in(splits[9], part), 71), part)
    prefix_kv = draw_prefix_kv(jax.random.fold_in(jax.random.fold_in(splits[9], part), 71), part)
    suffix_kv = scatter_about(part_splits[2], (PARENTS, CAP, 2, SUF, KVH * HD), 1.0, 4.5, ((0, 16),))
    counts = uneven_parts(part_splits[3], PARENTS, ROWS, CAP, 2).astype(jnp.int32)
    residual = draw_residual(jax.random.fold_in(jax.random.fold_in(splits[9], part), 71), part)
    out_weight = scatter_about(splits[5], (D, D), (D // 64) ** -0.5, 0.5, ((1, 16),))
    norm_gain = jnp.clip(1.0 + 0.18 * jax.random.normal(splits[6], (D,), jnp.float32), 0.1, 1.9)
    qkv_weight = scatter_about(splits[7], (D, QCOLS), D ** -0.5, 0.0625, ((1, 16),))
    owners = draw_owners(jax.random.fold_in(splits[9], 71), part)
    return dict(queries=queries, prefix_kv=prefix_kv, suffix_kv=suffix_kv, counts=counts, residual=residual, out_weight=out_weight, norm_gain=norm_gain, qkv_weight=qkv_weight, owners=owners)


def reference(queries, prefix_kv, suffix_kv, counts, residual, out_weight, norm_gain, qkv_weight, owners):
    score_scale = HD ** (-0.5)
    slot_rows = jnp.arange(CAP, dtype=jnp.int32)

    def one_parent(packed):
        query_rows, prefix_block, suffix_block, live_count = packed
        query_heads = query_rows.reshape(CAP, KVH, GQ, HD).astype(jnp.float32)
        prefix_keys = prefix_block[0].reshape(CTX, KVH, HD).astype(jnp.float32)
        prefix_values = prefix_block[1].reshape(CTX, KVH, HD).astype(jnp.float32)
        suffix_keys = suffix_block[:, 0].reshape(CAP, SUF, KVH, HD).astype(jnp.float32)
        suffix_values = suffix_block[:, 1].reshape(CAP, SUF, KVH, HD).astype(jnp.float32)
        distant = jnp.einsum('rgqd,tgd->rgqt', query_heads, prefix_keys) * score_scale
        nearby = jnp.einsum('rgqd,rsgd->rgqs', query_heads, suffix_keys) * score_scale
        highest = jnp.maximum(lax.optimization_barrier(jnp.max(distant, axis=-1)), lax.optimization_barrier(jnp.max(nearby, axis=-1)))[..., None]
        distant_exp = jnp.exp(distant - highest)
        nearby_exp = jnp.exp(nearby - highest)
        denominator = lax.optimization_barrier(jnp.sum(distant_exp, axis=-1, keepdims=True)) + lax.optimization_barrier(jnp.sum(nearby_exp, axis=-1, keepdims=True))
        distant_probs = lax.optimization_barrier((distant_exp / denominator).astype(jnp.bfloat16)).astype(jnp.float32)
        nearby_probs = lax.optimization_barrier((nearby_exp / denominator).astype(jnp.bfloat16)).astype(jnp.float32)
        mixed_heads = jnp.einsum('rgqt,tgd->rgqd', distant_probs, prefix_values)
        mixed_heads = mixed_heads + jnp.einsum('rgqs,rsgd->rgqd', nearby_probs, suffix_values)
        mixed_heads = mixed_heads.astype(jnp.bfloat16)
        is_valid = (slot_rows < live_count)[:, None, None, None]
        mixed_heads = jnp.where(is_valid, mixed_heads, jnp.zeros_like(mixed_heads))
        return mixed_heads.reshape(CAP, D)
    attended = lax.map(one_parent, (queries, prefix_kv, suffix_kv, counts)).reshape(SLOTS, D)
    stream = (residual.astype(jnp.float32) + jnp.dot(attended, out_weight, preferred_element_type=jnp.float32)).astype(jnp.bfloat16)
    stream_wide = stream.astype(jnp.float32)
    inverse = lax.rsqrt(lax.optimization_barrier(jnp.mean(stream_wide * stream_wide, axis=1, keepdims=True)) + 1e-05)
    normed = (stream_wide * inverse * norm_gain[None, :]).astype(jnp.bfloat16)
    projected = jnp.dot(normed, qkv_weight, preferred_element_type=jnp.float32).astype(jnp.bfloat16)
    slot_valid = (slot_rows[None, :] < counts[:, None]).reshape(SLOTS, 1)
    projected = jnp.where(slot_valid, projected, jnp.zeros_like(projected))
    device_ids = jnp.arange(N_WIDE, dtype=jnp.int32)
    member = owners[None, :, :] == device_ids[:, None, None]
    ranking = jnp.cumsum(member.astype(jnp.int32), axis=1) - 1
    slot_ids = jnp.arange(OWN_G, dtype=jnp.int32)
    chosen = member[:, None, :, :] & (ranking[:, None, :, :] == slot_ids[None, :, None, None])
    blocks = projected.reshape(PARENTS, CAP, KVH, GCOLS).astype(jnp.float32)
    regrouped = jnp.einsum('ejpg,prgf->ejrgf', chosen.astype(jnp.float32), blocks)
    return regrouped.astype(jnp.bfloat16)
```

```python
import functools

import jax
import jax.numpy as jnp
from jax import lax
from jax.experimental import pallas as pl
from jax.experimental.pallas import tpu as pltpu
from jax.sharding import PartitionSpec as P

KVH = 8
HD = 128
D = 8192
GQ = 8
GCOLS = 1280
CTX = 1024
SUF = 64
CAP = 12
OWN_G = 2
LIVE = 8
PAD = 16
GROUP_COLS = GQ * HD
HALF = D // 2
HALF_GROUPS = KVH // 2
KC = 512
MESH = pl.DeviceIdType.MESH
BF16 = jnp.bfloat16
F32 = jnp.float32


def kernel(
    n,
    q_ref, prefix_hbm, suffix_hbm, counts_ref, residual_ref, w1_hbm, gain_ref, w2_hbm, owners_ref,
    out_ref,
    qs, prefix, suffix, w1, w2, swap_out, swap_in, att, acc1, own_rows, acc2, send_buf, recv_buf,
    load_sem, swap_sem, att_send, att_recv, str_send, str_recv, a2a_send, a2a_recv,
):
    chips = n // 2
    zs = chips // 2
    me = lax.axis_index("wide")
    core = lax.rem(me, 2)
    chip = me // 2
    yi = lax.rem(chip, 2)
    zi = chip // 2
    sib = me + 1 - 2 * core
    live = n * LIVE
    cols1 = w1.shape[1]
    half_cols = HALF_GROUPS * HD

    halves = (1 - core, core)
    loads = []
    for i, half in enumerate(halves):
        cols = pl.ds(pl.multiple_of(half * half_cols, half_cols), half_cols)
        a = pltpu.make_async_copy(
            prefix_hbm.at[0, :, :, cols], prefix.at[i], load_sem.at[2 * i]
        )
        b = pltpu.make_async_copy(
            suffix_hbm.at[0, :, :, :, cols], suffix.at[i], load_sem.at[2 * i + 1]
        )
        a.start()
        b.start()
        loads.append((a, b))
    load_w1 = pltpu.make_async_copy(w1_hbm, w1, load_sem.at[4])
    load_w2 = pltpu.make_async_copy(w2_hbm, w2, load_sem.at[5])
    load_w1.start()
    load_w2.start()

    barrier = pltpu.get_barrier_semaphore()
    for off in range(1, n):
        pl.semaphore_signal(
            barrier, inc=1, device_id={"wide": lax.rem(me + off, n)}, device_id_type=MESH
        )

    qs[...] = jnp.zeros_like(qs)
    qs[0:CAP, :] = q_ref[0]
    live_count = counts_ref[me]
    slot_valid = lax.broadcasted_iota(jnp.int32, (PAD, HD), 0) < live_count
    rows = GQ * PAD
    suf_cols = CAP * SUF
    suf_mask = (
        lax.rem(lax.broadcasted_iota(jnp.int32, (rows, suf_cols), 0), PAD)
        == lax.broadcasted_iota(jnp.int32, (rows, suf_cols), 1) // SUF
    )
    scale = HD ** (-0.5)
    nt = (((1,), (1,)), ((), ()))

    def attend(i, half, target):
        for gg in range(HALF_GROUPS):
            base = half * HALF + gg * GROUP_COLS
            pieces = []
            for q in range(GQ):
                col = pl.multiple_of(base + q * HD, HD)
                pieces.append(qs[:, pl.ds(col, HD)])
            query = jnp.concatenate(pieces, axis=0)
            cols = slice(gg * HD, (gg + 1) * HD)
            keys = prefix[i, 0, :, cols]
            values = prefix[i, 1, :, cols]
            near_keys = suffix[i, :, 0, :, cols].reshape(suf_cols, HD)
            near_values = suffix[i, :, 1, :, cols].reshape(suf_cols, HD)
            far = lax.dot_general(query, keys, nt, preferred_element_type=F32) * scale
            near = lax.dot_general(query, near_keys, nt, preferred_element_type=F32) * scale
            near = jnp.where(suf_mask, near, -1e30)
            top = jnp.maximum(
                jnp.max(far, axis=1, keepdims=True), jnp.max(near, axis=1, keepdims=True)
            )
            far = jnp.exp(far - top)
            near = jnp.exp(near - top)
            total = jnp.sum(far, axis=1, keepdims=True) + jnp.sum(near, axis=1, keepdims=True)
            mixed = jnp.dot(far.astype(BF16), values, preferred_element_type=F32)
            mixed = mixed + jnp.dot(near.astype(BF16), near_values, preferred_element_type=F32)
            mixed = mixed / total
            for q in range(GQ):
                part = jnp.where(slot_valid, mixed[q * PAD:(q + 1) * PAD, :], 0.0)
                col = gg * GROUP_COLS + q * HD
                target[:, col:col + HD] = part.astype(BF16)

    loads[0][0].wait()
    loads[0][1].wait()
    attend(0, halves[0], swap_out)
    pl.semaphore_wait(barrier, n - 1)
    swap = pltpu.make_async_remote_copy(
        src_ref=swap_out, dst_ref=swap_in.at[1], send_sem=swap_sem.at[0], recv_sem=swap_sem.at[1],
        device_id={"wide": sib}, device_id_type=MESH,
    )
    swap.start()
    loads[1][0].wait()
    loads[1][1].wait()
    attend(1, halves[1], swap_in.at[0])

    pair_i = lax.broadcasted_iota(jnp.int32, (2 * CAP, 2 * PAD), 0)
    pair_j = lax.broadcasted_iota(jnp.int32, (2 * CAP, 2 * PAD), 1)
    from_core = pair_i // CAP
    wanted = jnp.where(from_core == core, 0, PAD) + lax.rem(pair_i, CAP)
    pick = (wanted == pair_j).astype(F32).astype(BF16)
    swap.wait_recv()
    for k in range(HALF // KC):
        cols = slice(k * KC, (k + 1) * KC)
        both = jnp.concatenate([swap_in[0, :, cols], swap_in[1, :, cols]], axis=0)
        att[core, chip, :, cols] = jnp.dot(pick, both, preferred_element_type=F32).astype(BF16)

    z_order = []
    for step in range(1, zs // 2 + 1):
        z_order.append(step)
        if zs - step != step:
            z_order.append(zs - step)

    def gather(buf, send_sems, recv_sems, arrived):
        started = []

        def push(slot_core, slot_chip, device):
            copy = pltpu.make_async_remote_copy(
                src_ref=buf.at[slot_core, slot_chip], dst_ref=buf.at[slot_core, slot_chip],
                send_sem=send_sems.at[len(started)], recv_sem=recv_sems.at[slot_core, slot_chip],
                device_id={"wide": device}, device_id_type=MESH,
            )
            copy.start()
            started.append(copy)

        def take(slot_core, slot_chip):
            pltpu.make_async_remote_copy(
                src_ref=buf.at[slot_core, slot_chip], dst_ref=buf.at[slot_core, slot_chip],
                send_sem=send_sems.at[0], recv_sem=recv_sems.at[slot_core, slot_chip],
                device_id={"wide": sib}, device_id_type=MESH,
            ).wait_recv()

        z_peers = [lax.rem(zi + step, zs) for step in z_order]
        other_y = (zi * 2 + 1 - yi) * 2 + core
        push(core, chip, other_y)
        for z in z_peers:
            push(core, chip, (z * 2 + yi) * 2 + core)
        push(core, chip, sib)
        arrived(core, chip)
        y_slots = [zi * 2 + 1 - yi] + [z * 2 + 1 - yi for z in z_peers]
        for k in range(zs):
            if k < zs - 1:
                slot = z_peers[k] * 2 + yi
                take(core, slot)
                push(core, slot, other_y)
                push(core, slot, sib)
                arrived(core, slot)
            take(core, y_slots[k])
            push(core, y_slots[k], sib)
            arrived(core, y_slots[k])
            slot = chip if k == 0 else z_peers[k - 1] * 2 + yi
            take(1 - core, slot)
            arrived(1 - core, slot)
        for slot in y_slots:
            take(1 - core, slot)
            arrived(1 - core, slot)
        return started

    started = gather(att, att_send, att_recv, lambda c, s: None)

    load_w1.wait()
    acc1[...] = residual_ref[...].astype(F32)
    per_half = HALF // KC

    @pl.loop(0, 2 * per_half)
    def _(step):
        half = step // per_half
        col = pl.multiple_of(lax.rem(step, per_half) * KC, KC)
        block = att[half, :, :, pl.ds(col, KC)].astype(F32).reshape(n * CAP, KC).astype(BF16)
        weight = w1[pl.ds(pl.multiple_of(step * KC, KC), KC), :]
        acc1[...] += jnp.dot(block, weight, preferred_element_type=F32)

    column = lax.broadcasted_iota(jnp.int32, (1, n * CAP), 1)
    parent = column // CAP
    slot = lax.rem(column, CAP)
    place = jnp.full((1, n * CAP), -1, jnp.int32)
    offset = jnp.int32(0)
    for p in range(n):
        count = counts_ref[p]
        place = jnp.where((parent == p) & (slot < count), slot + offset, place)
        offset = offset + count
    compact = (lax.broadcasted_iota(jnp.int32, (live, n * CAP), 0) == place).astype(F32).astype(BF16)
    stream = acc1[...].astype(BF16)
    own_rows_value = jnp.dot(compact, stream, preferred_element_type=F32).astype(BF16)
    own_rows[core, chip] = own_rows_value

    load_w2.wait()
    acc2[...] = jnp.zeros_like(acc2)
    squares = [jnp.zeros((live, 128), F32)]

    def project(slot_core, slot_chip):
        col = pl.multiple_of((slot_chip * 2 + slot_core) * cols1, cols1)
        block = own_rows[slot_core, slot_chip].astype(F32)
        for k in range(cols1 // 128):
            piece = block[:, k * 128:(k + 1) * 128]
            squares[0] = squares[0] + piece * piece
        scaled = (block * gain_ref[0:1, pl.ds(col, cols1)]).astype(BF16)
        acc2[...] += jnp.dot(scaled, w2[pl.ds(col, cols1), :], preferred_element_type=F32)

    started += gather(own_rows, str_send, str_recv, project)
    inverse = lax.rsqrt(jnp.sum(squares[0], axis=1, keepdims=True) / D + 1e-05)
    projected = (acc2[...] * inverse).astype(BF16)

    kv_group = me // (n // KVH)
    lines = n * OWN_G * CAP
    line = lax.broadcasted_iota(jnp.int32, (1, lines), 1)
    line_owner = line // (OWN_G * CAP)
    line_rank = lax.rem(line // CAP, OWN_G)
    line_slot = lax.rem(line, CAP)
    seen = jnp.zeros((1, lines), jnp.int32)
    place = jnp.full((1, lines), -1, jnp.int32)
    offset = jnp.int32(0)
    for p in range(n):
        count = counts_ref[p]
        member = line_owner == owners_ref[p, kv_group]
        hit = member & (seen == line_rank) & (line_slot < count)
        place = jnp.where(hit, line_slot + offset, place)
        seen = seen + member.astype(jnp.int32)
        offset = offset + count
    chosen = (lax.broadcasted_iota(jnp.int32, (live, lines), 0) == place).astype(F32)
    chosen = chosen.T.astype(BF16)
    outgoing = jnp.dot(chosen, projected, preferred_element_type=F32)
    for e in range(n):
        send_buf[e] = outgoing[e * OWN_G * CAP:(e + 1) * OWN_G * CAP, :].astype(BF16)
    for off in range(1, n):
        target = lax.rem(me + off, n)
        copy = pltpu.make_async_remote_copy(
            src_ref=send_buf.at[target], dst_ref=recv_buf.at[me],
            send_sem=a2a_send.at[off], recv_sem=a2a_recv.at[me],
            device_id={"wide": target}, device_id_type=MESH,
        )
        copy.start()
        started.append(copy)
    out_ref[me] = send_buf[me]
    for off in range(1, n):
        source = lax.rem(me + off, n)
        pltpu.make_async_remote_copy(
            src_ref=send_buf.at[source], dst_ref=recv_buf.at[source],
            send_sem=a2a_send.at[off], recv_sem=a2a_recv.at[source],
            device_id={"wide": source}, device_id_type=MESH,
        ).wait_recv()
        out_ref[source] = recv_buf[source]
    swap.wait_send()
    for copy in started:
        copy.wait_send()


def body(
    queries, prefix_kv, suffix_kv, counts, residual, out_weight, norm_gain, qkv_weight, owners
):
    n = lax.axis_size("wide")
    chips = n // 2
    cols1 = out_weight.shape[1]
    cols2 = qkv_weight.shape[1]
    half_cols = HALF_GROUPS * HD
    live = n * LIVE
    vmem = pl.BlockSpec(memory_space=pltpu.VMEM)
    smem = pl.BlockSpec(memory_space=pltpu.SMEM)
    anywhere = pl.BlockSpec(memory_space=pl.ANY)
    dma = pltpu.SemaphoreType.DMA
    received = pl.pallas_call(
        functools.partial(kernel, n),
        out_shape=jax.ShapeDtypeStruct((n, OWN_G * CAP, cols2), BF16),
        in_specs=[vmem, anywhere, anywhere, smem, vmem, anywhere, vmem, anywhere, smem],
        out_specs=vmem,
        scratch_shapes=[
            pltpu.VMEM((PAD, D), BF16),
            pltpu.VMEM((2, 2, CTX, half_cols), BF16),
            pltpu.VMEM((2, CAP, 2, SUF, half_cols), BF16),
            pltpu.VMEM((D, cols1), BF16),
            pltpu.VMEM((D, cols2), BF16),
            pltpu.VMEM((PAD, HALF), BF16),
            pltpu.VMEM((2, PAD, HALF), BF16),
            pltpu.VMEM((2, chips, 2 * CAP, HALF), BF16),
            pltpu.VMEM((n * CAP, cols1), F32),
            pltpu.VMEM((2, chips, live, cols1), BF16),
            pltpu.VMEM((live, cols2), F32),
            pltpu.VMEM((n, OWN_G * CAP, cols2), BF16),
            pltpu.VMEM((n, OWN_G * CAP, cols2), BF16),
            dma((6,)),
            dma((2,)),
            dma((n,)),
            dma((2, chips)),
            dma((n,)),
            dma((2, chips)),
            dma((n,)),
            dma((n,)),
        ],
        compiler_params=pltpu.CompilerParams(
            collective_id=0, has_side_effects=True, vmem_limit_bytes=60 * 1024 * 1024
        ),
    )(
        queries, prefix_kv, suffix_kv, counts, residual, out_weight, norm_gain[None, :],
        qkv_weight, owners,
    )
    received = received.reshape(KVH, n // KVH, OWN_G * CAP, cols2)
    return received.transpose(2, 0, 1, 3).reshape(1, OWN_G, CAP, KVH, GCOLS)


def solution(mesh):
    placed = (
        P(("groups", "wide"), None, None),
        P(("groups", "wide"), None, None, None),
        P(("groups", "wide"), None, None, None, None),
        P("groups"),
        P("groups", "wide"),
        P(None, "wide"),
        P(),
        P(None, "wide"),
        P(),
    )
    return jax.shard_map(
        body,
        mesh=mesh,
        in_specs=placed,
        out_specs=P(("groups", "wide"), None, None, None, None),
        check_vma=False,
    )
```

```python
import functools

import jax
import jax.numpy as jnp
from jax import lax
from jax.experimental import pallas as pl
from jax.experimental.pallas import tpu as pltpu
from jax.sharding import PartitionSpec as P

KVH = 8
HD = 128
D = 8192
GQ = 8
GCOLS = 1280
CTX = 1024
SUF = 64
CAP = 12
OWN_G = 2
LIVE = 8
PAD = 16
GROUP_COLS = GQ * HD
HALF = D // 2
HALF_GROUPS = KVH // 2
KC = 512
MESH = pl.DeviceIdType.MESH
BF16 = jnp.bfloat16
F32 = jnp.float32


def kernel(
    n,
    q_ref, prefix_hbm, suffix_hbm, counts_ref, residual_ref, w1_hbm, gain_ref, w2_hbm, owners_ref,
    out_ref,
    qs, mixed_rows, prefix, suffix, w1, w2, swap_out, swap_in, att, acc1, own_rows, acc2, send_buf,
    recv_buf,
    load_sem, swap_send, swap_recv, att_send, att_recv, str_send, str_recv, a2a_send, a2a_recv,
):
    zs = n // 4
    me = lax.axis_index("wide")
    core = lax.rem(me, 2)
    chip = me // 2
    yi = lax.rem(chip, 2)
    zi = chip // 2
    sib = me + 1 - 2 * core
    live = n * LIVE
    cols1 = w1.shape[1]
    half_cols = HALF_GROUPS * HD
    pieces, _, _, _, piece_cols = own_rows.shape

    halves = (1 - core, core)
    loads = []
    for i, half in enumerate(halves):
        cols = pl.ds(pl.multiple_of(half * half_cols, half_cols), half_cols)
        a = pltpu.make_async_copy(
            prefix_hbm.at[0, :, :, cols], prefix.at[i], load_sem.at[2 * i]
        )
        b = pltpu.make_async_copy(
            suffix_hbm.at[0, :, :, :, cols], suffix.at[i], load_sem.at[2 * i + 1]
        )
        a.start()
        b.start()
        loads.append((a, b))
    load_w1 = pltpu.make_async_copy(w1_hbm, w1, load_sem.at[4])
    load_w2 = pltpu.make_async_copy(w2_hbm, w2, load_sem.at[5])
    load_w1.start()
    load_w2.start()

    barrier = pltpu.get_barrier_semaphore()
    for off in range(1, n):
        pl.semaphore_signal(
            barrier, inc=1, device_id={"wide": lax.rem(me + off, n)}, device_id_type=MESH
        )

    z_order = []
    for step in range(1, zs // 2 + 1):
        z_order.append(step)
        if zs - step != step:
            z_order.append(zs - step)
    z_peers = [lax.rem(zi + step, zs) for step in z_order]
    other_y = (zi * 2 + 1 - yi) * 2 + core
    z_slots = [z * 2 + yi for z in z_peers]
    y_slots = [zi * 2 + 1 - yi] + [z * 2 + 1 - yi for z in z_peers]
    started = []

    def push(buf, sems, piece, which, slot_core, slot_chip, device):
        copy = pltpu.make_async_remote_copy(
            src_ref=buf.at[piece, slot_core, slot_chip],
            dst_ref=buf.at[piece, slot_core, slot_chip],
            send_sem=sems[0].at[piece, which], recv_sem=sems[1].at[piece, slot_core, slot_chip],
            device_id={"wide": device}, device_id_type=MESH,
        )
        copy.start()
        started.append(copy)

    def take(buf, sems, piece, slot_core, slot_chip):
        pltpu.make_async_remote_copy(
            src_ref=buf.at[piece, slot_core, slot_chip],
            dst_ref=buf.at[piece, slot_core, slot_chip],
            send_sem=sems[0].at[piece, 0], recv_sem=sems[1].at[piece, slot_core, slot_chip],
            device_id={"wide": sib}, device_id_type=MESH,
        ).wait_recv()

    def push_own(buf, sems, piece):
        push(buf, sems, piece, 0, core, chip, other_y)
        for k, slot in enumerate(z_slots):
            push(buf, sems, piece, 1 + k, core, chip, slot * 2 + core)
        push(buf, sems, piece, zs, core, chip, sib)

    def pass_z(buf, sems, piece, k):
        take(buf, sems, piece, core, z_slots[k])
        push(buf, sems, piece, zs + 1 + 2 * k, core, z_slots[k], other_y)
        push(buf, sems, piece, zs + 2 + 2 * k, core, z_slots[k], sib)

    def pass_y(buf, sems, piece, k):
        take(buf, sems, piece, core, y_slots[k])
        push(buf, sems, piece, 3 * zs - 1 + k, core, y_slots[k], sib)

    for g in range(KVH):
        for q in range(GQ):
            col = (g * GQ + q) * HD
            qs[g, pl.ds(q, CAP, stride=GQ), :] = q_ref[0, :, col:col + HD].astype(F32)
    mixed_rows[...] = jnp.zeros_like(mixed_rows)
    live_count = counts_ref[me]
    slot_valid = lax.broadcasted_iota(jnp.int32, (PAD, HD), 0) < live_count
    rows = CAP * GQ
    suf_cols = CAP * SUF
    suf_mask = (
        lax.broadcasted_iota(jnp.int32, (rows, suf_cols), 0) // GQ
        == lax.broadcasted_iota(jnp.int32, (rows, suf_cols), 1) // SUF
    )
    scale = HD ** (-0.5) * 1.4426950408889634
    nt = (((1,), (1,)), ((), ()))

    def attend(i, half, gg, target):
        query = qs[half * HALF_GROUPS + gg].astype(BF16)
        cols = slice(gg * HD, (gg + 1) * HD)
        keys = prefix[i, 0, :, cols]
        values = prefix[i, 1, :, cols]
        near_keys = suffix[i, :, 0, :, cols].reshape(suf_cols, HD)
        near_values = suffix[i, :, 1, :, cols].reshape(suf_cols, HD)
        far = lax.dot_general(query, keys, nt, preferred_element_type=F32)
        every = lax.dot_general(query, near_keys, nt, preferred_element_type=F32)
        near = jnp.concatenate(
            [every[r * GQ:(r + 1) * GQ, r * SUF:(r + 1) * SUF] for r in range(CAP)], axis=0
        )
        top = jnp.maximum(
            jnp.max(far, axis=1, keepdims=True), jnp.max(near, axis=1, keepdims=True)
        )
        far = jnp.exp2((far - top) * scale)
        near = jnp.exp2((near - top) * scale)
        total = jnp.sum(far, axis=1, keepdims=True) + jnp.sum(near, axis=1, keepdims=True)
        mixed = jnp.dot(far.astype(BF16), values, preferred_element_type=F32)
        spread = jnp.where(suf_mask, jnp.concatenate([near] * CAP, axis=1), 0.0).astype(BF16)
        mixed = mixed + jnp.dot(spread, near_values, preferred_element_type=F32)
        mixed_rows[0:rows, :] = mixed / total
        for q in range(GQ):
            part = jnp.where(slot_valid, mixed_rows[pl.ds(q, PAD, stride=GQ), :], 0.0)
            target[:, q * HD:(q + 1) * HD] = part.astype(BF16)

    pair_i = lax.broadcasted_iota(jnp.int32, (2 * CAP, 2 * PAD), 0)
    pair_j = lax.broadcasted_iota(jnp.int32, (2 * CAP, 2 * PAD), 1)
    from_core = pair_i // CAP
    wanted = jnp.where(from_core == core, 0, PAD) + lax.rem(pair_i, CAP)
    pick = (wanted == pair_j).astype(F32).astype(BF16)

    att_sems = (att_send, att_recv)
    for gg in range(HALF_GROUPS):
        if gg == 0:
            loads[0][0].wait()
            loads[0][1].wait()
        attend(0, halves[0], gg, swap_out.at[gg])
        if gg == 0:
            pl.semaphore_wait(barrier, n - 1)
        swap = pltpu.make_async_remote_copy(
            src_ref=swap_out.at[gg], dst_ref=swap_in.at[1, gg], send_sem=swap_send.at[gg],
            recv_sem=swap_recv.at[gg], device_id={"wide": sib}, device_id_type=MESH,
        )
        swap.start()
        started.append(swap)
        if gg == 0:
            loads[1][0].wait()
            loads[1][1].wait()
        attend(1, halves[1], gg, swap_in.at[0, gg])
        swap.wait_recv()
        both = jnp.concatenate([swap_in[0, gg], swap_in[1, gg]], axis=0)
        att[gg, core, chip] = jnp.dot(pick, both, preferred_element_type=F32).astype(BF16)
        push_own(att, att_sems, gg)

    acc1[...] = residual_ref[...].astype(F32)

    def forward(gg):
        for k in range(zs):
            if k < zs - 1:
                pass_z(att, att_sems, gg, k)
            pass_y(att, att_sems, gg, k)

    def out_project(gg):
        for slot in [chip] + z_slots + y_slots:
            take(att, att_sems, gg, 1 - core, slot)

        @pl.loop(0, 2 * GROUP_COLS // KC)
        def _(step):
            half = step // (GROUP_COLS // KC)
            col = pl.multiple_of(lax.rem(step, GROUP_COLS // KC) * KC, KC)
            block = att[gg, half, :, :, pl.ds(col, KC)].astype(F32)
            block = block.reshape(n * CAP, KC).astype(BF16)
            row = pl.multiple_of(half * HALF + gg * GROUP_COLS + col, KC)
            acc1[...] += jnp.dot(block, w1[pl.ds(row, KC), :], preferred_element_type=F32)

    forward(0)
    load_w1.wait()
    for gg in range(HALF_GROUPS):
        if gg + 1 < HALF_GROUPS:
            forward(gg + 1)
        out_project(gg)

    column = lax.broadcasted_iota(jnp.int32, (1, n * CAP), 1)
    parent = column // CAP
    slot = lax.rem(column, CAP)
    place = jnp.full((1, n * CAP), -1, jnp.int32)
    offset = jnp.int32(0)
    for p in range(n):
        count = counts_ref[p]
        place = jnp.where((parent == p) & (slot < count), slot + offset, place)
        offset = offset + count
    compact = (lax.broadcasted_iota(jnp.int32, (live, n * CAP), 0) == place).astype(F32).astype(BF16)
    stream = acc1[...].astype(BF16)
    str_sems = (str_send, str_recv)
    for piece in range(pieces):
        part = stream[:, piece * piece_cols:(piece + 1) * piece_cols]
        own_rows[piece, core, chip] = jnp.dot(
            compact, part, preferred_element_type=F32
        ).astype(BF16)
        push_own(own_rows, str_sems, piece)

    load_w2.wait()
    acc2[...] = jnp.zeros_like(acc2)
    squares = [jnp.zeros((live, 128), F32)]

    def project(piece, slot_core, slot_chip):
        col = (slot_chip * 2 + slot_core) * cols1 + piece * piece_cols
        cols = pl.ds(pl.multiple_of(col, piece_cols), piece_cols)
        block = own_rows[piece, slot_core, slot_chip].astype(F32)
        for k in range(piece_cols // 128):
            part = block[:, k * 128:(k + 1) * 128]
            squares[0] = squares[0] + part * part
        scaled = (block * gain_ref[0:1, cols]).astype(BF16)
        acc2[...] += jnp.dot(scaled, w2[cols, :], preferred_element_type=F32)

    for piece in range(pieces):
        project(piece, core, chip)
    for k in range(zs):
        for piece in range(pieces):
            if k < zs - 1:
                pass_z(own_rows, str_sems, piece, k)
            pass_y(own_rows, str_sems, piece, k)
        for piece in range(pieces):
            if k < zs - 1:
                project(piece, core, z_slots[k])
            project(piece, core, y_slots[k])
            slot = chip if k == 0 else z_slots[k - 1]
            take(own_rows, str_sems, piece, 1 - core, slot)
            project(piece, 1 - core, slot)
    for slot in y_slots:
        for piece in range(pieces):
            take(own_rows, str_sems, piece, 1 - core, slot)
            project(piece, 1 - core, slot)
    inverse = lax.rsqrt(jnp.sum(squares[0], axis=1, keepdims=True) / D + 1e-05)
    projected = (acc2[...] * inverse).astype(BF16)

    kv_group = me // (n // KVH)
    lines = n * OWN_G * CAP
    line = lax.broadcasted_iota(jnp.int32, (1, lines), 1)
    line_owner = line // (OWN_G * CAP)
    line_rank = lax.rem(line // CAP, OWN_G)
    line_slot = lax.rem(line, CAP)
    seen = jnp.zeros((1, lines), jnp.int32)
    place = jnp.full((1, lines), -1, jnp.int32)
    offset = jnp.int32(0)
    for p in range(n):
        count = counts_ref[p]
        member = line_owner == owners_ref[kv_group, p]
        hit = member & (seen == line_rank) & (line_slot < count)
        place = jnp.where(hit, line_slot + offset, place)
        seen = seen + member.astype(jnp.int32)
        offset = offset + count
    chosen = (lax.broadcasted_iota(jnp.int32, (live, lines), 0) == place).astype(F32)
    chosen = chosen.T.astype(BF16)
    outgoing = jnp.dot(chosen, projected, preferred_element_type=F32)
    for e in range(n):
        send_buf[e] = outgoing[e * OWN_G * CAP:(e + 1) * OWN_G * CAP, :].astype(BF16)
    for off in range(1, n):
        target = lax.rem(me + off, n)
        copy = pltpu.make_async_remote_copy(
            src_ref=send_buf.at[target], dst_ref=recv_buf.at[me],
            send_sem=a2a_send.at[off], recv_sem=a2a_recv.at[me],
            device_id={"wide": target}, device_id_type=MESH,
        )
        copy.start()
        started.append(copy)
    out_ref[me] = send_buf[me]
    for off in range(1, n):
        source = lax.rem(me + n - off, n)
        pltpu.make_async_remote_copy(
            src_ref=send_buf.at[source], dst_ref=recv_buf.at[source],
            send_sem=a2a_send.at[off], recv_sem=a2a_recv.at[source],
            device_id={"wide": source}, device_id_type=MESH,
        ).wait_recv()
        out_ref[source] = recv_buf[source]
    for copy in started:
        copy.wait_send()


def body(
    queries, prefix_kv, suffix_kv, counts, residual, out_weight, norm_gain, qkv_weight, owners
):
    n = lax.axis_size("wide")
    chips = n // 2
    cols1 = out_weight.shape[1]
    cols2 = qkv_weight.shape[1]
    half_cols = HALF_GROUPS * HD
    live = n * LIVE
    pieces = max(1, cols1 // 256)
    vmem = pl.BlockSpec(memory_space=pltpu.VMEM)
    smem = pl.BlockSpec(memory_space=pltpu.SMEM)
    anywhere = pl.BlockSpec(memory_space=pl.ANY)
    dma = pltpu.SemaphoreType.DMA
    received = pl.pallas_call(
        functools.partial(kernel, n),
        out_shape=jax.ShapeDtypeStruct((n, OWN_G * CAP, cols2), BF16),
        in_specs=[vmem, anywhere, anywhere, smem, vmem, anywhere, vmem, anywhere, smem],
        out_specs=vmem,
        scratch_shapes=[
            pltpu.VMEM((KVH, CAP * GQ, HD), F32),
            pltpu.VMEM((PAD * GQ, HD), F32),
            pltpu.VMEM((2, 2, CTX, half_cols), BF16),
            pltpu.VMEM((2, CAP, 2, SUF, half_cols), BF16),
            pltpu.VMEM((D, cols1), BF16),
            pltpu.VMEM((D, cols2), BF16),
            pltpu.VMEM((HALF_GROUPS, PAD, GROUP_COLS), BF16),
            pltpu.VMEM((2, HALF_GROUPS, PAD, GROUP_COLS), BF16),
            pltpu.VMEM((HALF_GROUPS, 2, chips, 2 * CAP, GROUP_COLS), BF16),
            pltpu.VMEM((n * CAP, cols1), F32),
            pltpu.VMEM((pieces, 2, chips, live, cols1 // pieces), BF16),
            pltpu.VMEM((live, cols2), F32),
            pltpu.VMEM((n, OWN_G * CAP, cols2), BF16),
            pltpu.VMEM((n, OWN_G * CAP, cols2), BF16),
            dma((6,)),
            dma((HALF_GROUPS,)),
            dma((HALF_GROUPS,)),
            dma((HALF_GROUPS, n)),
            dma((HALF_GROUPS, 2, chips)),
            dma((pieces, n)),
            dma((pieces, 2, chips)),
            dma((n,)),
            dma((n,)),
        ],
        compiler_params=pltpu.CompilerParams(
            collective_id=0, has_side_effects=True, vmem_limit_bytes=60 * 1024 * 1024
        ),
    )(
        queries, prefix_kv, suffix_kv, counts, residual, out_weight, norm_gain[None, :],
        qkv_weight, owners.T,
    )
    received = received.reshape(KVH, n // KVH, OWN_G * CAP, cols2)
    return received.transpose(2, 0, 1, 3).reshape(1, OWN_G, CAP, KVH, GCOLS)


def solution(mesh):
    placed = (
        P(("groups", "wide"), None, None),
        P(("groups", "wide"), None, None, None),
        P(("groups", "wide"), None, None, None, None),
        P("groups"),
        P("groups", "wide"),
        P(None, "wide"),
        P(),
        P(None, "wide"),
        P(),
    )
    return jax.shard_map(
        body,
        mesh=mesh,
        in_specs=placed,
        out_specs=P(("groups", "wide"), None, None, None, None),
        check_vma=False,
    )
```

```python
import functools

import jax
import jax.numpy as jnp
from jax import lax
from jax.experimental import pallas as pl
from jax.experimental.pallas import tpu as pltpu
from jax.sharding import PartitionSpec as P

KVH = 8
HD = 128
D = 8192
GQ = 8
GCOLS = 1280
CTX = 1024
SUF = 64
CAP = 12
OWN_G = 2
LIVE = 8
PAD = 16
GROUP_COLS = GQ * HD
HALF = D // 2
HALF_GROUPS = KVH // 2
KC = 1024
PIECE_GROUPS = 2
ATT_PIECES = HALF_GROUPS // PIECE_GROUPS
PIECE_COLS = PIECE_GROUPS * GROUP_COLS
MESH = pl.DeviceIdType.MESH
BF16 = jnp.bfloat16
F32 = jnp.float32


def kernel(
    n,
    q_ref, prefix_hbm, suffix_hbm, counts_ref, residual_ref, w1_hbm, gain_ref, w2_hbm, owners_ref,
    out_ref,
    qs, mixed_rows, prefix, suffix, w1, w2, swap_out, swap_in, att, acc1, own_rows, acc2, send_buf,
    recv_buf,
    load_sem, swap_send, swap_recv, att_send, att_recv, str_send, str_recv, a2a_send, a2a_recv,
):
    zs = n // 4
    me = lax.axis_index("wide")
    core = lax.rem(me, 2)
    chip = me // 2
    yi = lax.rem(chip, 2)
    zi = chip // 2
    sib = me + 1 - 2 * core
    live = n * LIVE
    cols1 = w1.shape[1]
    half_cols = HALF_GROUPS * HD

    halves = (1 - core, core)
    loads = []
    for i, half in enumerate(halves):
        cols = pl.ds(pl.multiple_of(half * half_cols, half_cols), half_cols)
        a = pltpu.make_async_copy(
            prefix_hbm.at[0, :, :, cols], prefix.at[i], load_sem.at[2 * i]
        )
        b = pltpu.make_async_copy(
            suffix_hbm.at[0, :, :, :, cols], suffix.at[i], load_sem.at[2 * i + 1]
        )
        a.start()
        b.start()
        loads.append((a, b))
    load_w1 = pltpu.make_async_copy(w1_hbm, w1, load_sem.at[4])
    load_w2 = pltpu.make_async_copy(w2_hbm, w2, load_sem.at[5])

    barrier = pltpu.get_barrier_semaphore()
    for off in range(1, n):
        pl.semaphore_signal(
            barrier, inc=1, device_id={"wide": lax.rem(me + off, n)}, device_id_type=MESH
        )

    z_order = []
    for step in range(1, zs // 2 + 1):
        z_order.append(step)
        if zs - step != step:
            z_order.append(zs - step)
    z_peers = [lax.rem(zi + step, zs) for step in z_order]
    if zs == 4:
        z_peers = [zi + 1 - 2 * lax.rem(zi, 2), 2 - zi // 2, 3 - 3 * (zi // 2)]
    other_y = (zi * 2 + 1 - yi) * 2 + core
    z_slots = [z * 2 + yi for z in z_peers]
    y_slots = [zi * 2 + 1 - yi] + [z * 2 + 1 - yi for z in z_peers]
    started = []

    def push(buf, sems, piece, which, slot_core, slot_chip, device):
        copy = pltpu.make_async_remote_copy(
            src_ref=buf.at[piece, slot_core, slot_chip],
            dst_ref=buf.at[piece, slot_core, slot_chip],
            send_sem=sems[0].at[piece, which], recv_sem=sems[1].at[piece, slot_core, slot_chip],
            device_id={"wide": device}, device_id_type=MESH,
        )
        copy.start()
        started.append(copy)

    def take(buf, sems, piece, slot_core, slot_chip):
        pltpu.make_async_remote_copy(
            src_ref=buf.at[piece, slot_core, slot_chip],
            dst_ref=buf.at[piece, slot_core, slot_chip],
            send_sem=sems[0].at[piece, 0], recv_sem=sems[1].at[piece, slot_core, slot_chip],
            device_id={"wide": sib}, device_id_type=MESH,
        ).wait_recv()

    def push_own(buf, sems, piece):
        push(buf, sems, piece, 0, core, chip, other_y)
        for k, slot in enumerate(z_slots):
            push(buf, sems, piece, 1 + k, core, chip, slot * 2 + core)
        push(buf, sems, piece, zs, core, chip, sib)

    def pass_z(buf, sems, piece, k):
        take(buf, sems, piece, core, z_slots[k])
        push(buf, sems, piece, zs + 1 + 2 * k, core, z_slots[k], other_y)
        push(buf, sems, piece, zs + 2 + 2 * k, core, z_slots[k], sib)

    def pass_y(buf, sems, piece, k):
        take(buf, sems, piece, core, y_slots[k])
        push(buf, sems, piece, 3 * zs - 1 + k, core, y_slots[k], sib)

    for g in range(KVH):
        for q in range(GQ):
            col = (g * GQ + q) * HD
            qs[g, pl.ds(q, CAP, stride=GQ), :] = q_ref[0, :, col:col + HD].astype(F32)
    mixed_rows[...] = jnp.zeros_like(mixed_rows)
    live_count = counts_ref[me]
    slot_valid = lax.broadcasted_iota(jnp.int32, (PAD, HD), 0) < live_count
    rows = CAP * GQ
    suf_cols = CAP * SUF
    suf_mask = (
        lax.broadcasted_iota(jnp.int32, (rows, suf_cols), 0) // GQ
        == lax.broadcasted_iota(jnp.int32, (rows, suf_cols), 1) // SUF
    )
    scale = HD ** (-0.5) * 1.4426950408889634
    nt = (((1,), (1,)), ((), ()))

    def attend(i, half, gg, target):
        query = qs[half * HALF_GROUPS + gg].astype(BF16)
        cols = slice(gg * HD, (gg + 1) * HD)
        keys = prefix[i, 0, :, cols]
        values = prefix[i, 1, :, cols]
        near_keys = suffix[i, :, 0, :, cols].reshape(suf_cols, HD)
        near_values = suffix[i, :, 1, :, cols].reshape(suf_cols, HD)
        far = lax.dot_general(query, keys, nt, preferred_element_type=F32)
        every = lax.dot_general(query, near_keys, nt, preferred_element_type=F32)
        near = jnp.concatenate(
            [every[r * GQ:(r + 1) * GQ, r * SUF:(r + 1) * SUF] for r in range(CAP)], axis=0
        )
        top = jnp.maximum(
            jnp.max(far, axis=1, keepdims=True), jnp.max(near, axis=1, keepdims=True)
        )
        far = jnp.exp2((far - top) * scale)
        near = jnp.exp2((near - top) * scale)
        total = jnp.sum(far, axis=1, keepdims=True) + jnp.sum(near, axis=1, keepdims=True)
        mixed = jnp.dot(far.astype(BF16), values, preferred_element_type=F32)
        spread = jnp.where(suf_mask, jnp.concatenate([near] * CAP, axis=1), 0.0).astype(BF16)
        mixed = mixed + jnp.dot(spread, near_values, preferred_element_type=F32)
        mixed_rows[0:rows, :] = mixed / total
        for q in range(GQ):
            part = jnp.where(slot_valid, mixed_rows[pl.ds(q, PAD, stride=GQ), :], 0.0)
            target[:, q * HD:(q + 1) * HD] = part.astype(BF16)

    pair_i = lax.broadcasted_iota(jnp.int32, (2 * CAP, 2 * PAD), 0)
    pair_j = lax.broadcasted_iota(jnp.int32, (2 * CAP, 2 * PAD), 1)
    from_core = pair_i // CAP
    wanted = jnp.where(from_core == core, 0, PAD) + lax.rem(pair_i, CAP)
    pick = (wanted == pair_j).astype(F32).astype(BF16)

    att_sems = (att_send, att_recv)
    for gg in range(HALF_GROUPS):
        if gg == 0:
            loads[0][0].wait()
            loads[0][1].wait()
        attend(0, halves[0], gg, swap_out.at[gg])
        if gg == 0:
            pl.semaphore_wait(barrier, n - 1)
        swap = pltpu.make_async_remote_copy(
            src_ref=swap_out.at[gg], dst_ref=swap_in.at[1, gg], send_sem=swap_send.at[gg],
            recv_sem=swap_recv.at[gg], device_id={"wide": sib}, device_id_type=MESH,
        )
        swap.start()
        started.append(swap)
        if gg == 0:
            loads[1][0].wait()
            loads[1][1].wait()
            load_w1.start()
            load_w2.start()
        attend(1, halves[1], gg, swap_in.at[0, gg])
        swap.wait_recv()
        both = jnp.concatenate([swap_in[0, gg], swap_in[1, gg]], axis=0)
        part = gg // PIECE_GROUPS
        col = gg % PIECE_GROUPS * GROUP_COLS
        att[part, core, chip, :, col:col + GROUP_COLS] = jnp.dot(
            pick, both, preferred_element_type=F32
        ).astype(BF16)
        if (gg + 1) % PIECE_GROUPS == 0:
            push_own(att, att_sems, part)

    acc1[...] = residual_ref[...].astype(F32)

    def forward(gg):
        for k in range(zs):
            if k < zs - 1:
                pass_z(att, att_sems, gg, k)
            pass_y(att, att_sems, gg, k)

    def out_project(gg):
        for slot in [chip] + z_slots + y_slots:
            take(att, att_sems, gg, 1 - core, slot)

        @pl.loop(0, 2 * PIECE_COLS // KC)
        def _(step):
            half = step // (PIECE_COLS // KC)
            col = pl.multiple_of(lax.rem(step, PIECE_COLS // KC) * KC, KC)
            block = att[gg, half, :, :, pl.ds(col, KC)].astype(F32)
            block = block.reshape(n * CAP, KC).astype(BF16)
            row = pl.multiple_of(half * HALF + gg * PIECE_COLS + col, KC)
            acc1[...] += jnp.dot(block, w1[pl.ds(row, KC), :], preferred_element_type=F32)

    forward(0)
    load_w1.wait()
    for gg in range(ATT_PIECES):
        if gg + 1 < ATT_PIECES:
            forward(gg + 1)
        out_project(gg)

    column = lax.broadcasted_iota(jnp.int32, (1, n * CAP), 1)
    parent = column // CAP
    slot = lax.rem(column, CAP)
    place = jnp.full((1, n * CAP), -1, jnp.int32)
    offset = jnp.int32(0)
    for p in range(n):
        count = counts_ref[p]
        place = jnp.where((parent == p) & (slot < count), slot + offset, place)
        offset = offset + count
    compact = (lax.broadcasted_iota(jnp.int32, (live, n * CAP), 0) == place).astype(F32).astype(BF16)
    stream = acc1[...].astype(BF16)
    str_sems = (str_send, str_recv)
    own_rows[0, core, chip] = jnp.dot(compact, stream, preferred_element_type=F32).astype(BF16)
    push_own(own_rows, str_sems, 0)

    load_w2.wait()
    acc2[...] = jnp.zeros_like(acc2)
    squares = [jnp.zeros((live, 128), F32)]

    def project(slot):
        take(own_rows, str_sems, 0, 1 - core, slot)
        base = slot * 2 * cols1
        cols = pl.ds(pl.multiple_of(base, 2 * cols1), 2 * cols1)
        block = jnp.concatenate(
            [own_rows[0, 0, slot].astype(F32), own_rows[0, 1, slot].astype(F32)], axis=1
        )
        for k in range(2 * cols1 // 128):
            part = block[:, k * 128:(k + 1) * 128]
            squares[0] = squares[0] + part * part
        scaled = (block * gain_ref[0:1, cols]).astype(BF16)
        acc2[...] += jnp.dot(scaled, w2[cols, :], preferred_element_type=F32)

    for k in range(zs):
        if k < zs - 1:
            pass_z(own_rows, str_sems, 0, k)
        pass_y(own_rows, str_sems, 0, k)
        if k == 0:
            project(chip)
        else:
            project(z_slots[k - 1])
            project(y_slots[k - 1])
    project(y_slots[zs - 1])
    inverse = lax.rsqrt(jnp.sum(squares[0], axis=1, keepdims=True) / D + 1e-05)
    projected = (acc2[...] * inverse).astype(BF16)

    kv_group = me // (n // KVH)
    lines = n * OWN_G * CAP
    line = lax.broadcasted_iota(jnp.int32, (1, lines), 1)
    line_owner = line // (OWN_G * CAP)
    line_rank = lax.rem(line // CAP, OWN_G)
    line_slot = lax.rem(line, CAP)
    seen = jnp.zeros((1, lines), jnp.int32)
    place = jnp.full((1, lines), -1, jnp.int32)
    offset = jnp.int32(0)
    for p in range(n):
        count = counts_ref[p]
        member = line_owner == owners_ref[kv_group, p]
        hit = member & (seen == line_rank) & (line_slot < count)
        place = jnp.where(hit, line_slot + offset, place)
        seen = seen + member.astype(jnp.int32)
        offset = offset + count
    chosen = (lax.broadcasted_iota(jnp.int32, (live, lines), 0) == place).astype(F32)
    chosen = chosen.T.astype(BF16)
    outgoing = jnp.dot(chosen, projected, preferred_element_type=F32)
    for e in range(n):
        send_buf[e] = outgoing[e * OWN_G * CAP:(e + 1) * OWN_G * CAP, :].astype(BF16)
    for off in range(1, n):
        target = lax.rem(me + off, n)
        copy = pltpu.make_async_remote_copy(
            src_ref=send_buf.at[target], dst_ref=recv_buf.at[me],
            send_sem=a2a_send.at[off], recv_sem=a2a_recv.at[me],
            device_id={"wide": target}, device_id_type=MESH,
        )
        copy.start()
        started.append(copy)
    out_ref[me] = send_buf[me]
    for off in range(1, n):
        source = lax.rem(me + n - off, n)
        pltpu.make_async_remote_copy(
            src_ref=send_buf.at[source], dst_ref=recv_buf.at[source],
            send_sem=a2a_send.at[off], recv_sem=a2a_recv.at[source],
            device_id={"wide": source}, device_id_type=MESH,
        ).wait_recv()
        out_ref[source] = recv_buf[source]
    for copy in started:
        copy.wait_send()


def body(
    queries, prefix_kv, suffix_kv, counts, residual, out_weight, norm_gain, qkv_weight, owners
):
    n = lax.axis_size("wide")
    chips = n // 2
    cols1 = out_weight.shape[1]
    cols2 = qkv_weight.shape[1]
    half_cols = HALF_GROUPS * HD
    live = n * LIVE
    vmem = pl.BlockSpec(memory_space=pltpu.VMEM)
    smem = pl.BlockSpec(memory_space=pltpu.SMEM)
    anywhere = pl.BlockSpec(memory_space=pl.ANY)
    dma = pltpu.SemaphoreType.DMA
    received = pl.pallas_call(
        functools.partial(kernel, n),
        out_shape=jax.ShapeDtypeStruct((n, OWN_G * CAP, cols2), BF16),
        in_specs=[vmem, anywhere, anywhere, smem, vmem, anywhere, vmem, anywhere, smem],
        out_specs=vmem,
        scratch_shapes=[
            pltpu.VMEM((KVH, CAP * GQ, HD), F32),
            pltpu.VMEM((PAD * GQ, HD), F32),
            pltpu.VMEM((2, 2, CTX, half_cols), BF16),
            pltpu.VMEM((2, CAP, 2, SUF, half_cols), BF16),
            pltpu.VMEM((D, cols1), BF16),
            pltpu.VMEM((D, cols2), BF16),
            pltpu.VMEM((HALF_GROUPS, PAD, GROUP_COLS), BF16),
            pltpu.VMEM((2, HALF_GROUPS, PAD, GROUP_COLS), BF16),
            pltpu.VMEM((ATT_PIECES, 2, chips, 2 * CAP, PIECE_COLS), BF16),
            pltpu.VMEM((n * CAP, cols1), F32),
            pltpu.VMEM((1, 2, chips, live, cols1), BF16),
            pltpu.VMEM((live, cols2), F32),
            pltpu.VMEM((n, OWN_G * CAP, cols2), BF16),
            pltpu.VMEM((n, OWN_G * CAP, cols2), BF16),
            dma((6,)),
            dma((HALF_GROUPS,)),
            dma((HALF_GROUPS,)),
            dma((ATT_PIECES, n)),
            dma((ATT_PIECES, 2, chips)),
            dma((1, n)),
            dma((1, 2, chips)),
            dma((n,)),
            dma((n,)),
        ],
        compiler_params=pltpu.CompilerParams(
            collective_id=0, has_side_effects=True, vmem_limit_bytes=60 * 1024 * 1024
        ),
    )(
        queries, prefix_kv, suffix_kv, counts, residual, out_weight, norm_gain[None, :],
        qkv_weight, owners.T,
    )
    received = received.reshape(KVH, n // KVH, OWN_G * CAP, cols2)
    return received.transpose(2, 0, 1, 3).reshape(1, OWN_G, CAP, KVH, GCOLS)


def solution(mesh):
    placed = (
        P(("groups", "wide"), None, None),
        P(("groups", "wide"), None, None, None),
        P(("groups", "wide"), None, None, None, None),
        P("groups"),
        P("groups", "wide"),
        P(None, "wide"),
        P(),
        P(None, "wide"),
        P(),
    )
    return jax.shard_map(
        body,
        mesh=mesh,
        in_specs=placed,
        out_specs=P(("groups", "wide"), None, None, None, None),
        check_vma=False,
    )
```

```python
import functools

import jax
import jax.numpy as jnp
from jax import lax
from jax.experimental import pallas as pl
from jax.experimental.pallas import tpu as pltpu
from jax.sharding import PartitionSpec as P

KVH = 8
HD = 128
D = 8192
GQ = 8
GCOLS = 1280
CTX = 1024
SUF = 64
CAP = 12
OWN_G = 2
LIVE = 8
PAD = 16
GROUP_COLS = GQ * HD
HALF = D // 2
HALF_GROUPS = KVH // 2
KC = 512
PIECE_GROUPS = 1
ATT_PIECES = HALF_GROUPS // PIECE_GROUPS
PIECE_COLS = PIECE_GROUPS * GROUP_COLS
MESH = pl.DeviceIdType.MESH
BF16 = jnp.bfloat16
F32 = jnp.float32


def kernel(
    n,
    q_hbm, prefix_hbm, suffix_hbm, counts_ref, residual_hbm, w1_hbm, gain_hbm, w2_hbm, owners_ref,
    out_ref,
    qs, mixed_rows, prefix, suffix, w1, w2, swap_out, swap_in, att, acc1, own_rows, acc2, send_buf,
    recv_buf,
    q_ref, residual_ref, gain_ref, compact_ref, chosen_ref,
    load_sem, swap_send, swap_recv, att_send, att_recv, str_send, str_recv, a2a_send, a2a_recv,
):
    zs = n // 4
    me = lax.axis_index("wide")
    core = lax.rem(me, 2)
    chip = me // 2
    yi = lax.rem(chip, 2)
    zi = chip // 2
    sib = me + 1 - 2 * core
    live = n * LIVE
    cols1 = w1.shape[1]
    half_cols = HALF_GROUPS * HD

    load_q = pltpu.make_async_copy(q_hbm, q_ref, load_sem.at[6])
    load_q.start()
    halves = (1 - core, core)
    loads = []
    for i, half in enumerate(halves):
        cols = pl.ds(pl.multiple_of(half * half_cols, half_cols), half_cols)
        a = pltpu.make_async_copy(
            prefix_hbm.at[0, :, :, cols], prefix.at[i], load_sem.at[2 * i]
        )
        b = pltpu.make_async_copy(
            suffix_hbm.at[0, :, :, :, cols], suffix.at[i], load_sem.at[2 * i + 1]
        )
        a.start()
        b.start()
        loads.append((a, b))
    load_residual = pltpu.make_async_copy(residual_hbm, residual_ref, load_sem.at[7])
    load_gain = pltpu.make_async_copy(gain_hbm, gain_ref, load_sem.at[8])
    load_residual.start()
    load_gain.start()
    load_w1 = pltpu.make_async_copy(w1_hbm, w1, load_sem.at[4])
    load_w2 = pltpu.make_async_copy(w2_hbm, w2, load_sem.at[5])

    barrier = pltpu.get_barrier_semaphore()
    for off in range(1, n):
        pl.semaphore_signal(
            barrier, inc=1, device_id={"wide": lax.rem(me + off, n)}, device_id_type=MESH
        )

    z_order = []
    for step in range(1, zs // 2 + 1):
        z_order.append(step)
        if zs - step != step:
            z_order.append(zs - step)
    z_peers = [lax.rem(zi + step, zs) for step in z_order]
    if zs == 4:
        z_peers = [zi + 1 - 2 * lax.rem(zi, 2), 2 - zi // 2, 3 - 3 * (zi // 2)]
    other_y = (zi * 2 + 1 - yi) * 2 + core
    z_slots = [z * 2 + yi for z in z_peers]
    y_slots = [zi * 2 + 1 - yi] + [z * 2 + 1 - yi for z in z_peers]
    started = []

    def push(buf, sems, piece, which, slot_core, slot_chip, device):
        copy = pltpu.make_async_remote_copy(
            src_ref=buf.at[piece, slot_core, slot_chip],
            dst_ref=buf.at[piece, slot_core, slot_chip],
            send_sem=sems[0].at[piece, which], recv_sem=sems[1].at[piece, slot_core, slot_chip],
            device_id={"wide": device}, device_id_type=MESH,
        )
        copy.start()
        started.append(copy)

    def take(buf, sems, piece, slot_core, slot_chip):
        pltpu.make_async_remote_copy(
            src_ref=buf.at[piece, slot_core, slot_chip],
            dst_ref=buf.at[piece, slot_core, slot_chip],
            send_sem=sems[0].at[piece, 0], recv_sem=sems[1].at[piece, slot_core, slot_chip],
            device_id={"wide": sib}, device_id_type=MESH,
        ).wait_recv()

    def push_own(buf, sems, piece):
        push(buf, sems, piece, 0, core, chip, other_y)
        for k, slot in enumerate(z_slots):
            push(buf, sems, piece, 1 + k, core, chip, slot * 2 + core)
        push(buf, sems, piece, zs, core, chip, sib)

    def pass_z(buf, sems, piece, k):
        take(buf, sems, piece, core, z_slots[k])
        push(buf, sems, piece, zs + 1 + 2 * k, core, z_slots[k], other_y)
        push(buf, sems, piece, zs + 2 + 2 * k, core, z_slots[k], sib)

    def pass_y(buf, sems, piece, k):
        take(buf, sems, piece, core, y_slots[k])
        push(buf, sems, piece, 3 * zs - 1 + k, core, y_slots[k], sib)

    load_q.wait()
    for g in range(KVH):
        for q in range(GQ):
            col = (g * GQ + q) * HD
            qs[g, pl.ds(q, CAP, stride=GQ), :] = q_ref[0, :, col:col + HD].astype(F32)
    mixed_rows[...] = jnp.zeros_like(mixed_rows)
    live_count = counts_ref[me]
    slot_valid = lax.broadcasted_iota(jnp.int32, (PAD, HD), 0) < live_count
    rows = CAP * GQ
    suf_cols = CAP * SUF
    suf_mask = (
        lax.broadcasted_iota(jnp.int32, (rows, suf_cols), 0) // GQ
        == lax.broadcasted_iota(jnp.int32, (rows, suf_cols), 1) // SUF
    )
    scale = HD ** (-0.5) * 1.4426950408889634
    nt = (((1,), (1,)), ((), ()))

    def attend(i, half, gg, target):
        query = qs[half * HALF_GROUPS + gg].astype(BF16)
        cols = slice(gg * HD, (gg + 1) * HD)
        keys = prefix[i, 0, :, cols]
        values = prefix[i, 1, :, cols]
        near_keys = suffix[i, :, 0, :, cols].reshape(suf_cols, HD)
        near_values = suffix[i, :, 1, :, cols].reshape(suf_cols, HD)
        far = lax.dot_general(query, keys, nt, preferred_element_type=F32)
        every = lax.dot_general(query, near_keys, nt, preferred_element_type=F32)
        near = jnp.concatenate(
            [every[r * GQ:(r + 1) * GQ, r * SUF:(r + 1) * SUF] for r in range(CAP)], axis=0
        )
        top = jnp.maximum(
            jnp.max(far, axis=1, keepdims=True), jnp.max(near, axis=1, keepdims=True)
        )
        far = jnp.exp2((far - top) * scale)
        near = jnp.exp2((near - top) * scale)
        total = jnp.sum(far, axis=1, keepdims=True) + jnp.sum(near, axis=1, keepdims=True)
        mixed = jnp.dot(far.astype(BF16), values, preferred_element_type=F32)
        spread = jnp.where(suf_mask, jnp.concatenate([near] * CAP, axis=1), 0.0).astype(BF16)
        mixed = mixed + jnp.dot(spread, near_values, preferred_element_type=F32)
        mixed_rows[0:rows, :] = mixed / total
        for q in range(GQ):
            part = jnp.where(slot_valid, mixed_rows[pl.ds(q, PAD, stride=GQ), :], 0.0)
            target[:, q * HD:(q + 1) * HD] = part.astype(BF16)

    pair_i = lax.broadcasted_iota(jnp.int32, (2 * CAP, 2 * PAD), 0)
    pair_j = lax.broadcasted_iota(jnp.int32, (2 * CAP, 2 * PAD), 1)
    from_core = pair_i // CAP
    wanted = jnp.where(from_core == core, 0, PAD) + lax.rem(pair_i, CAP)
    pick = (wanted == pair_j).astype(F32).astype(BF16)

    att_sems = (att_send, att_recv)
    for gg in range(HALF_GROUPS):
        if gg == 0:
            loads[0][0].wait()
            loads[0][1].wait()
        attend(0, halves[0], gg, swap_out.at[gg])
        if gg == 0:
            pl.semaphore_wait(barrier, n - 1)
        swap = pltpu.make_async_remote_copy(
            src_ref=swap_out.at[gg], dst_ref=swap_in.at[1, gg], send_sem=swap_send.at[gg],
            recv_sem=swap_recv.at[gg], device_id={"wide": sib}, device_id_type=MESH,
        )
        swap.start()
        started.append(swap)
        if gg == 0:
            loads[1][0].wait()
            loads[1][1].wait()
            load_w1.start()
            load_w2.start()
        attend(1, halves[1], gg, swap_in.at[0, gg])
        swap.wait_recv()
        both = jnp.concatenate([swap_in[0, gg], swap_in[1, gg]], axis=0)
        part = gg // PIECE_GROUPS
        col = gg % PIECE_GROUPS * GROUP_COLS
        att[part, core, chip, :, col:col + GROUP_COLS] = jnp.dot(
            pick, both, preferred_element_type=F32
        ).astype(BF16)
        if (gg + 1) % PIECE_GROUPS == 0:
            push_own(att, att_sems, part)

    column = lax.broadcasted_iota(jnp.int32, (1, n * CAP), 1)
    parent = column // CAP
    slot = lax.rem(column, CAP)
    place = jnp.full((1, n * CAP), -1, jnp.int32)
    offset = jnp.int32(0)
    for p in range(n):
        count = counts_ref[p]
        place = jnp.where((parent == p) & (slot < count), slot + offset, place)
        offset = offset + count
    compact = lax.broadcasted_iota(jnp.int32, (live, n * CAP), 0) == place
    compact_ref[...] = compact.astype(F32).astype(BF16)

    load_residual.wait()
    load_gain.wait()
    acc1[...] = residual_ref[...].astype(F32)

    steps = 2 * PIECE_COLS // KC

    def forward(gg, k):
        if k < zs - 1:
            pass_z(att, att_sems, gg, k)
        pass_y(att, att_sems, gg, k)

    def out_project(gg, step):
        half = step // (steps // 2)
        col = step % (steps // 2) * KC
        block = att[gg, half, :, :, col:col + KC].astype(F32)
        block = block.reshape(n * CAP, KC).astype(BF16)
        row = half * HALF + gg * PIECE_COLS + col
        acc1[...] += jnp.dot(block, w1[row:row + KC, :], preferred_element_type=F32)

    for k in range(zs):
        forward(0, k)
    load_w1.wait()
    for gg in range(ATT_PIECES):
        for slot in [chip] + z_slots + y_slots:
            take(att, att_sems, gg, 1 - core, slot)
        step = 0
        if gg + 1 < ATT_PIECES:
            for k in range(zs):
                forward(gg + 1, k)
                if step < steps:
                    out_project(gg, step)
                    step += 1
        while step < steps:
            out_project(gg, step)
            step += 1

    stream = acc1[...].astype(BF16)
    str_sems = (str_send, str_recv)
    own_rows[0, core, chip] = jnp.dot(compact_ref[...], stream, preferred_element_type=F32).astype(BF16)
    push_own(own_rows, str_sems, 0)

    kv_group = me // (n // KVH)
    lines = n * OWN_G * CAP
    line = lax.broadcasted_iota(jnp.int32, (1, lines), 1)
    line_owner = line // (OWN_G * CAP)
    line_rank = lax.rem(line // CAP, OWN_G)
    line_slot = lax.rem(line, CAP)
    seen = jnp.zeros((1, lines), jnp.int32)
    place = jnp.full((1, lines), -1, jnp.int32)
    offset = jnp.int32(0)
    for p in range(n):
        count = counts_ref[p]
        member = line_owner == owners_ref[kv_group, p]
        hit = member & (seen == line_rank) & (line_slot < count)
        place = jnp.where(hit, line_slot + offset, place)
        seen = seen + member.astype(jnp.int32)
        offset = offset + count
    chosen = (lax.broadcasted_iota(jnp.int32, (live, lines), 0) == place).astype(F32)
    chosen_ref[...] = chosen.T.astype(BF16)

    load_w2.wait()
    acc2[...] = jnp.zeros_like(acc2)
    squares = [jnp.zeros((live, 128), F32)]

    def project(slot):
        take(own_rows, str_sems, 0, 1 - core, slot)
        base = slot * 2 * cols1
        cols = pl.ds(pl.multiple_of(base, 2 * cols1), 2 * cols1)
        block = jnp.concatenate(
            [own_rows[0, 0, slot].astype(F32), own_rows[0, 1, slot].astype(F32)], axis=1
        )
        for k in range(2 * cols1 // 128):
            part = block[:, k * 128:(k + 1) * 128]
            squares[0] = squares[0] + part * part
        scaled = (block * gain_ref[0:1, cols]).astype(BF16)
        acc2[...] += jnp.dot(scaled, w2[cols, :], preferred_element_type=F32)

    for k in range(zs):
        if k < zs - 1:
            pass_z(own_rows, str_sems, 0, k)
        pass_y(own_rows, str_sems, 0, k)
        if k == 0:
            project(chip)
        else:
            project(z_slots[k - 1])
            project(y_slots[k - 1])
    project(y_slots[zs - 1])
    inverse = lax.rsqrt(jnp.sum(squares[0], axis=1, keepdims=True) / D + 1e-05)
    projected = (acc2[...] * inverse).astype(BF16)

    outgoing = jnp.dot(chosen_ref[...], projected, preferred_element_type=F32)
    for e in range(n):
        send_buf[e] = outgoing[e * OWN_G * CAP:(e + 1) * OWN_G * CAP, :].astype(BF16)
    for off in range(1, n):
        target = lax.rem(me + off, n)
        copy = pltpu.make_async_remote_copy(
            src_ref=send_buf.at[target], dst_ref=recv_buf.at[me],
            send_sem=a2a_send.at[off], recv_sem=a2a_recv.at[me],
            device_id={"wide": target}, device_id_type=MESH,
        )
        copy.start()
        started.append(copy)
    out_ref[me] = send_buf[me]
    for off in range(1, n):
        source = lax.rem(me + n - off, n)
        pltpu.make_async_remote_copy(
            src_ref=send_buf.at[source], dst_ref=recv_buf.at[source],
            send_sem=a2a_send.at[off], recv_sem=a2a_recv.at[source],
            device_id={"wide": source}, device_id_type=MESH,
        ).wait_recv()
        out_ref[source] = recv_buf[source]
    for copy in started:
        copy.wait_send()


def body(
    queries, prefix_kv, suffix_kv, counts, residual, out_weight, norm_gain, qkv_weight, owners
):
    n = lax.axis_size("wide")
    chips = n // 2
    cols1 = out_weight.shape[1]
    cols2 = qkv_weight.shape[1]
    half_cols = HALF_GROUPS * HD
    live = n * LIVE
    vmem = pl.BlockSpec(memory_space=pltpu.VMEM)
    smem = pl.BlockSpec(memory_space=pltpu.SMEM)
    anywhere = pl.BlockSpec(memory_space=pl.ANY)
    dma = pltpu.SemaphoreType.DMA
    received = pl.pallas_call(
        functools.partial(kernel, n),
        out_shape=jax.ShapeDtypeStruct((n, OWN_G * CAP, cols2), BF16),
        in_specs=[anywhere] * 3 + [smem] + [anywhere] * 4 + [smem],
        out_specs=vmem,
        scratch_shapes=[
            pltpu.VMEM((KVH, CAP * GQ, HD), F32),
            pltpu.VMEM((PAD * GQ, HD), F32),
            pltpu.VMEM((2, 2, CTX, half_cols), BF16),
            pltpu.VMEM((2, CAP, 2, SUF, half_cols), BF16),
            pltpu.VMEM((D, cols1), BF16),
            pltpu.VMEM((D, cols2), BF16),
            pltpu.VMEM((HALF_GROUPS, PAD, GROUP_COLS), BF16),
            pltpu.VMEM((2, HALF_GROUPS, PAD, GROUP_COLS), BF16),
            pltpu.VMEM((ATT_PIECES, 2, chips, 2 * CAP, PIECE_COLS), BF16),
            pltpu.VMEM((n * CAP, cols1), F32),
            pltpu.VMEM((1, 2, chips, live, cols1), BF16),
            pltpu.VMEM((live, cols2), F32),
            pltpu.VMEM((n, OWN_G * CAP, cols2), BF16),
            pltpu.VMEM((n, OWN_G * CAP, cols2), BF16),
            pltpu.VMEM(queries.shape, BF16),
            pltpu.VMEM(residual.shape, BF16),
            pltpu.VMEM((1, D), F32),
            pltpu.VMEM((live, n * CAP), BF16),
            pltpu.VMEM((n * OWN_G * CAP, live), BF16),
            dma((9,)),
            dma((HALF_GROUPS,)),
            dma((HALF_GROUPS,)),
            dma((ATT_PIECES, n)),
            dma((ATT_PIECES, 2, chips)),
            dma((1, n)),
            dma((1, 2, chips)),
            dma((n,)),
            dma((n,)),
        ],
        compiler_params=pltpu.CompilerParams(
            collective_id=0, has_side_effects=True, vmem_limit_bytes=60 * 1024 * 1024
        ),
    )(
        queries, prefix_kv, suffix_kv, counts, residual, out_weight, norm_gain[None, :],
        qkv_weight, owners.T,
    )
    received = received.reshape(KVH, n // KVH, OWN_G * CAP, cols2)
    return received.transpose(2, 0, 1, 3).reshape(1, OWN_G, CAP, KVH, GCOLS)


def solution(mesh):
    placed = (
        P(("groups", "wide"), None, None),
        P(("groups", "wide"), None, None, None),
        P(("groups", "wide"), None, None, None, None),
        P("groups"),
        P("groups", "wide"),
        P(None, "wide"),
        P(),
        P(None, "wide"),
        P(),
    )
    return jax.shard_map(
        body,
        mesh=mesh,
        in_specs=placed,
        out_specs=P(("groups", "wide"), None, None, None, None),
        check_vma=False,
    )
```

```python
import functools

import jax
import jax.numpy as jnp
from jax import lax
from jax.experimental import pallas as pl
from jax.experimental.pallas import tpu as pltpu
from jax.sharding import PartitionSpec as P

KVH = 8
HD = 128
D = 8192
GQ = 8
GCOLS = 1280
CTX = 1024
SUF = 64
CAP = 12
OWN_G = 2
LIVE = 8
PAD = 16
GROUP_COLS = GQ * HD
HALF = D // 2
HALF_GROUPS = KVH // 2
KC = 512
MESH = pl.DeviceIdType.MESH
BF16 = jnp.bfloat16
F32 = jnp.float32


def kernel(
    n,
    q_hbm, prefix_hbm, suffix_hbm, counts_ref, residual_hbm, w1_hbm, gain_hbm, w2_hbm, owners_ref,
    out_ref,
    qs, mixed_rows, prefix, suffix, w1, w2, swap_out, swap_in, att, acc1, own_rows, acc2, send_buf,
    recv_buf,
    q_ref, residual_ref, gain_ref, compact_ref, chosen_ref,
    load_sem, swap_sem, att_send, att_recv, att_line, str_send, str_recv, str_line, a2a_send,
    a2a_recv,
):
    zs = n // 4
    me = lax.axis_index("wide")
    core = lax.rem(me, 2)
    chip = me // 2
    yi = lax.rem(chip, 2)
    zi = chip // 2
    sib = me + 1 - 2 * core
    live = n * LIVE
    cols1 = w1.shape[1]
    half_cols = HALF_GROUPS * HD

    load_q = pltpu.make_async_copy(q_hbm, q_ref, load_sem.at[6])
    load_q.start()
    halves = (1 - core, core)
    loads = []
    for i, half in enumerate(halves):
        cols = pl.ds(pl.multiple_of(half * half_cols, half_cols), half_cols)
        a = pltpu.make_async_copy(
            prefix_hbm.at[0, :, :, cols], prefix.at[i], load_sem.at[2 * i]
        )
        b = pltpu.make_async_copy(
            suffix_hbm.at[0, :, :, :, cols], suffix.at[i], load_sem.at[2 * i + 1]
        )
        a.start()
        b.start()
        loads.append((a, b))
    load_residual = pltpu.make_async_copy(residual_hbm, residual_ref, load_sem.at[7])
    load_gain = pltpu.make_async_copy(gain_hbm, gain_ref, load_sem.at[8])
    load_residual.start()
    load_gain.start()
    load_w1 = pltpu.make_async_copy(w1_hbm, w1, load_sem.at[4])
    load_w2 = pltpu.make_async_copy(w2_hbm, w2, load_sem.at[5])

    barrier = pltpu.get_barrier_semaphore()
    for off in range(1, n):
        pl.semaphore_signal(
            barrier, inc=1, device_id={"wide": lax.rem(me + off, n)}, device_id_type=MESH
        )

    z_order = []
    for step in range(1, zs // 2 + 1):
        z_order.append(step)
        if zs - step != step:
            z_order.append(zs - step)
    z_peers = [lax.rem(zi + step, zs) for step in z_order]
    if zs == 4:
        z_peers = [zi + 1 - 2 * lax.rem(zi, 2), 2 - zi // 2, 3 - 3 * (zi // 2)]
    other_y = (zi * 2 + 1 - yi) * 2 + core
    lines_z = [zi] + z_peers
    started = []

    def copy_of(block, send, recv, device):
        return pltpu.make_async_remote_copy(
            src_ref=block, dst_ref=block, send_sem=send, recv_sem=recv,
            device_id={"wide": device}, device_id_type=MESH,
        )

    def launch(copy):
        copy.start()
        started.append(copy)

    def push_own(buf, sends, recvs):
        block = buf.at[core, yi, zi]
        launch(copy_of(block, sends.at[0], recvs.at[yi, zi], other_y))
        for k, z in enumerate(z_peers):
            launch(copy_of(block, sends.at[1 + k], recvs.at[yi, zi], (z * 2 + yi) * 2 + core))

    def pass_z(buf, sends, recvs):
        for k, z in enumerate(z_peers):
            block = buf.at[core, yi, z]
            copy_of(block, sends.at[0], recvs.at[yi, z], other_y).wait_recv()
            launch(copy_of(block, sends.at[zs + k], recvs.at[yi, z], other_y))

    def take_y(buf, sends, recvs, z):
        copy_of(buf.at[core, 1 - yi, z], sends.at[0], recvs.at[1 - yi, z], other_y).wait_recv()

    def push_line(buf, sends, recvs, y, which):
        launch(copy_of(buf.at[core, y], sends.at[2 * zs - 1 + which], recvs.at[which], sib))

    def take_line(buf, sends, recvs, y, which):
        copy_of(buf.at[1 - core, y], sends.at[0], recvs.at[which], sib).wait_recv()

    load_q.wait()
    for g in range(KVH):
        for q in range(GQ):
            col = (g * GQ + q) * HD
            qs[g, pl.ds(q, CAP, stride=GQ), :] = q_ref[0, :, col:col + HD].astype(F32)
    mixed_rows[...] = jnp.zeros_like(mixed_rows)
    live_count = counts_ref[me]
    slot_valid = lax.broadcasted_iota(jnp.int32, (PAD, HD), 0) < live_count
    rows = CAP * GQ
    suf_cols = CAP * SUF
    suf_mask = (
        lax.broadcasted_iota(jnp.int32, (rows, suf_cols), 0) // GQ
        == lax.broadcasted_iota(jnp.int32, (rows, suf_cols), 1) // SUF
    )
    scale = HD ** (-0.5) * 1.4426950408889634
    nt = (((1,), (1,)), ((), ()))

    def attend(i, half, gg, target):
        query = qs[half * HALF_GROUPS + gg].astype(BF16)
        cols = slice(gg * HD, (gg + 1) * HD)
        keys = prefix[i, 0, :, cols]
        values = prefix[i, 1, :, cols]
        near_keys = suffix[i, :, 0, :, cols].reshape(suf_cols, HD)
        near_values = suffix[i, :, 1, :, cols].reshape(suf_cols, HD)
        far = lax.dot_general(query, keys, nt, preferred_element_type=F32)
        every = lax.dot_general(query, near_keys, nt, preferred_element_type=F32)
        near = jnp.concatenate(
            [every[r * GQ:(r + 1) * GQ, r * SUF:(r + 1) * SUF] for r in range(CAP)], axis=0
        )
        top = jnp.maximum(
            jnp.max(far, axis=1, keepdims=True), jnp.max(near, axis=1, keepdims=True)
        )
        far = jnp.exp2((far - top) * scale)
        near = jnp.exp2((near - top) * scale)
        total = jnp.sum(far, axis=1, keepdims=True) + jnp.sum(near, axis=1, keepdims=True)
        mixed = jnp.dot(far.astype(BF16), values, preferred_element_type=F32)
        spread = jnp.where(suf_mask, jnp.concatenate([near] * CAP, axis=1), 0.0).astype(BF16)
        mixed = mixed + jnp.dot(spread, near_values, preferred_element_type=F32)
        mixed_rows[0:rows, :] = mixed / total
        for q in range(GQ):
            part = jnp.where(slot_valid, mixed_rows[pl.ds(q, PAD, stride=GQ), :], 0.0)
            target[:, q * HD:(q + 1) * HD] = part.astype(BF16)

    pair_i = lax.broadcasted_iota(jnp.int32, (2 * CAP, 2 * PAD), 0)
    pair_j = lax.broadcasted_iota(jnp.int32, (2 * CAP, 2 * PAD), 1)
    from_core = pair_i // CAP
    wanted = jnp.where(from_core == core, 0, PAD) + lax.rem(pair_i, CAP)
    pick = (wanted == pair_j).astype(F32).astype(BF16)

    loads[0][0].wait()
    loads[0][1].wait()
    for gg in range(HALF_GROUPS):
        attend(0, halves[0], gg, swap_out.at[gg])
    pl.semaphore_wait(barrier, n - 1)
    swap = pltpu.make_async_remote_copy(
        src_ref=swap_out, dst_ref=swap_in.at[1], send_sem=swap_sem.at[0], recv_sem=swap_sem.at[1],
        device_id={"wide": sib}, device_id_type=MESH,
    )
    launch(swap)
    loads[1][0].wait()
    loads[1][1].wait()
    load_w1.start()
    load_w2.start()
    for gg in range(HALF_GROUPS):
        attend(1, halves[1], gg, swap_in.at[0, gg])
    swap.wait_recv()
    for gg in range(HALF_GROUPS):
        both = jnp.concatenate([swap_in[0, gg], swap_in[1, gg]], axis=0)
        att[core, yi, zi, :, gg * GROUP_COLS:(gg + 1) * GROUP_COLS] = jnp.dot(
            pick, both, preferred_element_type=F32
        ).astype(BF16)
    push_own(att, att_send, att_recv)

    column = lax.broadcasted_iota(jnp.int32, (1, n * CAP), 1)
    place_chip = column // (2 * CAP)
    place_chip = lax.rem(place_chip, zs) * 2 + place_chip // zs
    parent = place_chip * 2 + lax.rem(column // CAP, 2)
    slot = lax.rem(column, CAP)
    place = jnp.full((1, n * CAP), -1, jnp.int32)
    offset = jnp.int32(0)
    for p in range(n):
        count = counts_ref[p]
        place = jnp.where((parent == p) & (slot < count), slot + offset, place)
        offset = offset + count
    compact = lax.broadcasted_iota(jnp.int32, (live, n * CAP), 0) == place
    compact_ref[...] = compact.astype(F32).astype(BF16)

    load_residual.wait()
    load_gain.wait()
    residual = residual_ref[...].astype(F32)
    for y in range(2):
        for z in range(zs):
            to, source = (y * zs + z) * 2 * CAP, (z * 2 + y) * 2 * CAP
            acc1[to:to + 2 * CAP, :] = residual[source:source + 2 * CAP, :]

    def out_project(half, y):
        line_rows = zs * 2 * CAP
        place = pl.ds(pl.multiple_of(y * line_rows, line_rows), line_rows)

        @pl.loop(0, HALF // KC)
        def _(step):
            col = pl.multiple_of(step * KC, KC)
            block = att[half, y, :, :, pl.ds(col, KC)].astype(F32)
            block = block.reshape(line_rows, KC).astype(BF16)
            row = pl.multiple_of(half * HALF + col, KC)
            acc1[place, :] += jnp.dot(block, w1[pl.ds(row, KC), :], preferred_element_type=F32)

    pass_z(att, att_send, att_recv)
    push_line(att, att_send, att_line, yi, 0)
    load_w1.wait()
    out_project(core, yi)
    take_line(att, att_send, att_line, yi, 0)
    out_project(1 - core, yi)
    for z in lines_z:
        take_y(att, att_send, att_recv, z)
    push_line(att, att_send, att_line, 1 - yi, 1)
    out_project(core, 1 - yi)
    take_line(att, att_send, att_line, 1 - yi, 1)
    out_project(1 - core, 1 - yi)

    stream = acc1[...].astype(BF16)
    own_rows[core, yi, zi] = jnp.dot(
        compact_ref[...], stream, preferred_element_type=F32
    ).astype(BF16)
    push_own(own_rows, str_send, str_recv)

    kv_group = me // (n // KVH)
    lines = n * OWN_G * CAP
    line = lax.broadcasted_iota(jnp.int32, (1, lines), 1)
    line_owner = line // (OWN_G * CAP)
    line_rank = lax.rem(line // CAP, OWN_G)
    line_slot = lax.rem(line, CAP)
    seen = jnp.zeros((1, lines), jnp.int32)
    place = jnp.full((1, lines), -1, jnp.int32)
    offset = jnp.int32(0)
    for p in range(n):
        count = counts_ref[p]
        member = line_owner == owners_ref[kv_group, p]
        hit = member & (seen == line_rank) & (line_slot < count)
        place = jnp.where(hit, line_slot + offset, place)
        seen = seen + member.astype(jnp.int32)
        offset = offset + count
    chosen = (lax.broadcasted_iota(jnp.int32, (live, lines), 0) == place).astype(F32)
    chosen_ref[...] = chosen.T.astype(BF16)

    load_w2.wait()
    acc2[...] = jnp.zeros_like(acc2)
    squares = [jnp.zeros((live, 128), F32)]

    def project(half, y, z):
        base = ((z * 2 + y) * 2 + half) * cols1
        cols = pl.ds(pl.multiple_of(base, cols1), cols1)
        block = own_rows[half, y, z].astype(F32)
        for k in range(cols1 // 128):
            part = block[:, k * 128:(k + 1) * 128]
            squares[0] = squares[0] + part * part
        scaled = (block * gain_ref[0:1, cols]).astype(BF16)
        acc2[...] += jnp.dot(scaled, w2[cols, :], preferred_element_type=F32)

    project(core, yi, zi)
    pass_z(own_rows, str_send, str_recv)
    push_line(own_rows, str_send, str_line, yi, 0)
    for z in z_peers:
        project(core, yi, z)
    take_line(own_rows, str_send, str_line, yi, 0)
    for z in lines_z:
        project(1 - core, yi, z)
    for z in lines_z:
        take_y(own_rows, str_send, str_recv, z)
    push_line(own_rows, str_send, str_line, 1 - yi, 1)
    for z in lines_z:
        project(core, 1 - yi, z)
    take_line(own_rows, str_send, str_line, 1 - yi, 1)
    for z in lines_z:
        project(1 - core, 1 - yi, z)
    inverse = lax.rsqrt(jnp.sum(squares[0], axis=1, keepdims=True) / D + 1e-05)
    projected = (acc2[...] * inverse).astype(BF16)

    outgoing = jnp.dot(chosen_ref[...], projected, preferred_element_type=F32)
    for e in range(n):
        send_buf[e] = outgoing[e * OWN_G * CAP:(e + 1) * OWN_G * CAP, :].astype(BF16)
    for off in range(1, n):
        target = lax.rem(me + off, n)
        copy = pltpu.make_async_remote_copy(
            src_ref=send_buf.at[target], dst_ref=recv_buf.at[me],
            send_sem=a2a_send.at[off], recv_sem=a2a_recv.at[me],
            device_id={"wide": target}, device_id_type=MESH,
        )
        copy.start()
        started.append(copy)
    out_ref[me] = send_buf[me]
    for off in range(1, n):
        source = lax.rem(me + n - off, n)
        pltpu.make_async_remote_copy(
            src_ref=send_buf.at[source], dst_ref=recv_buf.at[source],
            send_sem=a2a_send.at[off], recv_sem=a2a_recv.at[source],
            device_id={"wide": source}, device_id_type=MESH,
        ).wait_recv()
        out_ref[source] = recv_buf[source]
    for copy in started:
        copy.wait_send()


def body(
    queries, prefix_kv, suffix_kv, counts, residual, out_weight, norm_gain, qkv_weight, owners
):
    n = lax.axis_size("wide")
    zs = n // 4
    cols1 = out_weight.shape[1]
    cols2 = qkv_weight.shape[1]
    half_cols = HALF_GROUPS * HD
    live = n * LIVE
    vmem = pl.BlockSpec(memory_space=pltpu.VMEM)
    smem = pl.BlockSpec(memory_space=pltpu.SMEM)
    anywhere = pl.BlockSpec(memory_space=pl.ANY)
    dma = pltpu.SemaphoreType.DMA
    received = pl.pallas_call(
        functools.partial(kernel, n),
        out_shape=jax.ShapeDtypeStruct((n, OWN_G * CAP, cols2), BF16),
        in_specs=[anywhere] * 3 + [smem] + [anywhere] * 4 + [smem],
        out_specs=vmem,
        scratch_shapes=[
            pltpu.VMEM((KVH, CAP * GQ, HD), F32),
            pltpu.VMEM((PAD * GQ, HD), F32),
            pltpu.VMEM((2, 2, CTX, half_cols), BF16),
            pltpu.VMEM((2, CAP, 2, SUF, half_cols), BF16),
            pltpu.VMEM((D, cols1), BF16),
            pltpu.VMEM((D, cols2), BF16),
            pltpu.VMEM((HALF_GROUPS, PAD, GROUP_COLS), BF16),
            pltpu.VMEM((2, HALF_GROUPS, PAD, GROUP_COLS), BF16),
            pltpu.VMEM((2, 2, zs, 2 * CAP, HALF), BF16),
            pltpu.VMEM((n * CAP, cols1), F32),
            pltpu.VMEM((2, 2, zs, live, cols1), BF16),
            pltpu.VMEM((live, cols2), F32),
            pltpu.VMEM((n, OWN_G * CAP, cols2), BF16),
            pltpu.VMEM((n, OWN_G * CAP, cols2), BF16),
            pltpu.VMEM(queries.shape, BF16),
            pltpu.VMEM(residual.shape, BF16),
            pltpu.VMEM((1, D), F32),
            pltpu.VMEM((live, n * CAP), BF16),
            pltpu.VMEM((n * OWN_G * CAP, live), BF16),
            dma((9,)),
            dma((2,)),
            dma((2 * zs + 1,)),
            dma((2, zs)),
            dma((2,)),
            dma((2 * zs + 1,)),
            dma((2, zs)),
            dma((2,)),
            dma((n,)),
            dma((n,)),
        ],
        compiler_params=pltpu.CompilerParams(
            collective_id=0, has_side_effects=True, vmem_limit_bytes=60 * 1024 * 1024
        ),
    )(
        queries, prefix_kv, suffix_kv, counts, residual, out_weight, norm_gain[None, :],
        qkv_weight, owners.T,
    )
    received = received.reshape(KVH, n // KVH, OWN_G * CAP, cols2)
    return received.transpose(2, 0, 1, 3).reshape(1, OWN_G, CAP, KVH, GCOLS)


def solution(mesh):
    placed = (
        P(("groups", "wide"), None, None),
        P(("groups", "wide"), None, None, None),
        P(("groups", "wide"), None, None, None, None),
        P("groups"),
        P("groups", "wide"),
        P(None, "wide"),
        P(),
        P(None, "wide"),
        P(),
    )
    return jax.shard_map(
        body,
        mesh=mesh,
        in_specs=placed,
        out_specs=P(("groups", "wide"), None, None, None, None),
        check_vma=False,
    )
```

```python
import functools

import jax
import jax.numpy as jnp
from jax import lax
from jax.experimental import pallas as pl
from jax.experimental.pallas import tpu as pltpu
from jax.sharding import PartitionSpec as P

KVH = 8
HD = 128
D = 8192
GQ = 8
GCOLS = 1280
CTX = 1024
SUF = 64
CAP = 12
OWN_G = 2
LIVE = 8
PAD = 16
GROUP_COLS = GQ * HD
HALF = D // 2
HALF_GROUPS = KVH // 2
KC = 512
MESH = pl.DeviceIdType.MESH
BF16 = jnp.bfloat16
F32 = jnp.float32


def kernel(
    n,
    q_hbm, prefix_hbm, suffix_hbm, counts_ref, residual_hbm, w1_hbm, gain_hbm, w2_hbm, owners_ref,
    out_ref,
    qs, mixed_rows, prefix, suffix, w1, w2, swap_out, swap_in, att, acc1, own_rows, acc2, send_buf,
    recv_buf,
    q_ref, residual_ref, gain_ref, compact_ref, chosen_ref,
    load_sem, swap_sem, att_send, att_recv, att_line, str_send, str_recv, str_line, a2a_send,
    a2a_recv,
):
    zs = n // 4
    me = lax.axis_index("wide")
    core = lax.rem(me, 2)
    chip = me // 2
    yi = lax.rem(chip, 2)
    zi = chip // 2
    sib = me + 1 - 2 * core
    live = n * LIVE
    cols1 = w1.shape[1]
    half_cols = HALF_GROUPS * HD

    load_q = pltpu.make_async_copy(q_hbm, q_ref, load_sem.at[6])
    load_q.start()
    halves = (1 - core, core)
    loads = []
    for i, half in enumerate(halves):
        cols = pl.ds(pl.multiple_of(half * half_cols, half_cols), half_cols)
        a = pltpu.make_async_copy(
            prefix_hbm.at[0, :, :, cols], prefix.at[i], load_sem.at[2 * i]
        )
        b = pltpu.make_async_copy(
            suffix_hbm.at[0, :, :, :, cols], suffix.at[i], load_sem.at[2 * i + 1]
        )
        a.start()
        b.start()
        loads.append((a, b))
    load_residual = pltpu.make_async_copy(residual_hbm, residual_ref, load_sem.at[7])
    load_gain = pltpu.make_async_copy(gain_hbm, gain_ref, load_sem.at[8])
    load_residual.start()
    load_gain.start()
    load_w1 = pltpu.make_async_copy(w1_hbm, w1, load_sem.at[4])
    load_w2 = pltpu.make_async_copy(w2_hbm, w2, load_sem.at[5])

    barrier = pltpu.get_barrier_semaphore()
    for off in range(1, n):
        pl.semaphore_signal(
            barrier, inc=1, device_id={"wide": lax.rem(me + off, n)}, device_id_type=MESH
        )

    other_y = (zi * 2 + 1 - yi) * 2 + core
    above, below = me + 4, me - 4
    has_above, has_below = zi < zs - 1, zi > 0
    started = []

    def copy_of(block, send, recv, device):
        return pltpu.make_async_remote_copy(
            src_ref=block, dst_ref=block, send_sem=send, recv_sem=recv,
            device_id={"wide": device}, device_id_type=MESH,
        )

    def launch(copy):
        copy.start()
        started.append(copy.wait_send)

    def launch_if(condition, make):
        pl.when(condition)(lambda: make().start())
        started.append(lambda: pl.when(condition)(lambda: make().wait_send()))

    def push_own(buf, sends, recvs):
        block, recv = buf.at[core, yi, zi], recvs.at[yi, zi]
        launch_if(has_above, lambda: copy_of(block, sends.at[0], recv, above))
        launch_if(has_below, lambda: copy_of(block, sends.at[1], recv, below))
        launch(copy_of(block, sends.at[2], recv, other_y))

    def line_steps(visit):
        for step in range(1, zs):
            visit(2 * step - 2, zi - step, zi >= step, has_above, above)
            visit(2 * step - 1, zi + step, zi + step < zs, has_below, below)

    def pass_z(buf, sends, recvs):
        def visit(index, z, there, onward, device):
            def copy(which, target):
                return copy_of(
                    buf.at[core, yi, z], sends.at[which], recvs.at[yi, z], target
                )

            pl.when(there)(lambda: copy(0, other_y).wait_recv())
            launch_if(there & onward, lambda: copy(3 + 2 * index, device))
            launch_if(there, lambda: copy(4 + 2 * index, other_y))

        line_steps(visit)

    def take_y(buf, sends, recvs):
        def take(z):
            copy_of(
                buf.at[core, 1 - yi, z], sends.at[0], recvs.at[1 - yi, z], other_y
            ).wait_recv()

        take(zi)
        line_steps(lambda index, z, there, onward, device: pl.when(there)(lambda: take(z)))

    def push_line(buf, sends, recvs, y, which):
        launch(copy_of(buf.at[core, y], sends.at[4 * zs - 1 + which], recvs.at[which], sib))

    def take_line(buf, sends, recvs, y, which):
        copy_of(buf.at[1 - core, y], sends.at[0], recvs.at[which], sib).wait_recv()

    load_q.wait()
    for g in range(KVH):
        for q in range(GQ):
            col = (g * GQ + q) * HD
            qs[g, pl.ds(q, CAP, stride=GQ), :] = q_ref[0, :, col:col + HD].astype(F32)
    mixed_rows[...] = jnp.zeros_like(mixed_rows)
    live_count = counts_ref[me]
    slot_valid = lax.broadcasted_iota(jnp.int32, (PAD, HD), 0) < live_count
    rows = CAP * GQ
    suf_cols = CAP * SUF
    suf_mask = (
        lax.broadcasted_iota(jnp.int32, (rows, suf_cols), 0) // GQ
        == lax.broadcasted_iota(jnp.int32, (rows, suf_cols), 1) // SUF
    )
    scale = HD ** (-0.5) * 1.4426950408889634
    nt = (((1,), (1,)), ((), ()))

    def attend(i, half, gg, target):
        query = qs[half * HALF_GROUPS + gg].astype(BF16)
        cols = slice(gg * HD, (gg + 1) * HD)
        keys = prefix[i, 0, :, cols]
        values = prefix[i, 1, :, cols]
        near_keys = suffix[i, :, 0, :, cols].reshape(suf_cols, HD)
        near_values = suffix[i, :, 1, :, cols].reshape(suf_cols, HD)
        far = lax.dot_general(query, keys, nt, preferred_element_type=F32)
        every = lax.dot_general(query, near_keys, nt, preferred_element_type=F32)
        near = jnp.concatenate(
            [every[r * GQ:(r + 1) * GQ, r * SUF:(r + 1) * SUF] for r in range(CAP)], axis=0
        )
        top = jnp.maximum(
            jnp.max(far, axis=1, keepdims=True), jnp.max(near, axis=1, keepdims=True)
        )
        far = jnp.exp2((far - top) * scale)
        near = jnp.exp2((near - top) * scale)
        total = jnp.sum(far, axis=1, keepdims=True) + jnp.sum(near, axis=1, keepdims=True)
        mixed = jnp.dot(far.astype(BF16), values, preferred_element_type=F32)
        spread = jnp.where(suf_mask, jnp.concatenate([near] * CAP, axis=1), 0.0).astype(BF16)
        mixed = mixed + jnp.dot(spread, near_values, preferred_element_type=F32)
        mixed_rows[0:rows, :] = mixed / total
        for q in range(GQ):
            part = jnp.where(slot_valid, mixed_rows[pl.ds(q, PAD, stride=GQ), :], 0.0)
            target[:, q * HD:(q + 1) * HD] = part.astype(BF16)

    pair_i = lax.broadcasted_iota(jnp.int32, (2 * CAP, 2 * PAD), 0)
    pair_j = lax.broadcasted_iota(jnp.int32, (2 * CAP, 2 * PAD), 1)
    from_core = pair_i // CAP
    wanted = jnp.where(from_core == core, 0, PAD) + lax.rem(pair_i, CAP)
    pick = (wanted == pair_j).astype(F32).astype(BF16)

    loads[0][0].wait()
    loads[0][1].wait()
    for gg in range(HALF_GROUPS):
        attend(0, halves[0], gg, swap_out.at[gg])
    pl.semaphore_wait(barrier, n - 1)
    swap = pltpu.make_async_remote_copy(
        src_ref=swap_out, dst_ref=swap_in.at[1], send_sem=swap_sem.at[0], recv_sem=swap_sem.at[1],
        device_id={"wide": sib}, device_id_type=MESH,
    )
    launch(swap)
    loads[1][0].wait()
    loads[1][1].wait()
    load_w1.start()
    load_w2.start()
    for gg in range(HALF_GROUPS):
        attend(1, halves[1], gg, swap_in.at[0, gg])
    swap.wait_recv()
    for gg in range(HALF_GROUPS):
        both = jnp.concatenate([swap_in[0, gg], swap_in[1, gg]], axis=0)
        att[core, yi, zi, :, gg * GROUP_COLS:(gg + 1) * GROUP_COLS] = jnp.dot(
            pick, both, preferred_element_type=F32
        ).astype(BF16)
    push_own(att, att_send, att_recv)

    column = lax.broadcasted_iota(jnp.int32, (1, n * CAP), 1)
    place_chip = column // (2 * CAP)
    place_chip = lax.rem(place_chip, zs) * 2 + place_chip // zs
    parent = place_chip * 2 + lax.rem(column // CAP, 2)
    slot = lax.rem(column, CAP)
    place = jnp.full((1, n * CAP), -1, jnp.int32)
    offset = jnp.int32(0)
    for p in range(n):
        count = counts_ref[p]
        place = jnp.where((parent == p) & (slot < count), slot + offset, place)
        offset = offset + count
    compact = lax.broadcasted_iota(jnp.int32, (live, n * CAP), 0) == place
    compact_ref[...] = compact.astype(F32).astype(BF16)

    load_residual.wait()
    load_gain.wait()
    residual = residual_ref[...].astype(F32)
    for y in range(2):
        for z in range(zs):
            to, source = (y * zs + z) * 2 * CAP, (z * 2 + y) * 2 * CAP
            acc1[to:to + 2 * CAP, :] = residual[source:source + 2 * CAP, :]

    def out_project(half, y):
        line_rows = zs * 2 * CAP
        place = pl.ds(pl.multiple_of(y * line_rows, line_rows), line_rows)

        @pl.loop(0, HALF // KC)
        def _(step):
            col = pl.multiple_of(step * KC, KC)
            block = att[half, y, :, :, pl.ds(col, KC)].astype(F32)
            block = block.reshape(line_rows, KC).astype(BF16)
            row = pl.multiple_of(half * HALF + col, KC)
            acc1[place, :] += jnp.dot(block, w1[pl.ds(row, KC), :], preferred_element_type=F32)

    pass_z(att, att_send, att_recv)
    push_line(att, att_send, att_line, yi, 0)
    load_w1.wait()
    out_project(core, yi)
    take_line(att, att_send, att_line, yi, 0)
    out_project(1 - core, yi)
    take_y(att, att_send, att_recv)
    push_line(att, att_send, att_line, 1 - yi, 1)
    out_project(core, 1 - yi)
    take_line(att, att_send, att_line, 1 - yi, 1)
    out_project(1 - core, 1 - yi)

    stream = acc1[...].astype(BF16)
    own_rows[core, yi, zi] = jnp.dot(
        compact_ref[...], stream, preferred_element_type=F32
    ).astype(BF16)
    push_own(own_rows, str_send, str_recv)

    kv_group = me // (n // KVH)
    lines = n * OWN_G * CAP
    line = lax.broadcasted_iota(jnp.int32, (1, lines), 1)
    line_owner = line // (OWN_G * CAP)
    line_rank = lax.rem(line // CAP, OWN_G)
    line_slot = lax.rem(line, CAP)
    seen = jnp.zeros((1, lines), jnp.int32)
    place = jnp.full((1, lines), -1, jnp.int32)
    offset = jnp.int32(0)
    for p in range(n):
        count = counts_ref[p]
        member = line_owner == owners_ref[kv_group, p]
        hit = member & (seen == line_rank) & (line_slot < count)
        place = jnp.where(hit, line_slot + offset, place)
        seen = seen + member.astype(jnp.int32)
        offset = offset + count
    chosen = (lax.broadcasted_iota(jnp.int32, (live, lines), 0) == place).astype(F32)
    chosen_ref[...] = chosen.T.astype(BF16)

    load_w2.wait()
    acc2[...] = jnp.zeros_like(acc2)
    squares = [jnp.zeros((live, 128), F32)]

    def project(half, y, z):
        base = ((z * 2 + y) * 2 + half) * cols1
        cols = pl.ds(pl.multiple_of(base, cols1), cols1)
        block = own_rows[half, y, z].astype(F32)
        for k in range(cols1 // 128):
            part = block[:, k * 128:(k + 1) * 128]
            squares[0] = squares[0] + part * part
        scaled = (block * gain_ref[0:1, cols]).astype(BF16)
        acc2[...] += jnp.dot(scaled, w2[cols, :], preferred_element_type=F32)

    project(core, yi, zi)
    pass_z(own_rows, str_send, str_recv)
    push_line(own_rows, str_send, str_line, yi, 0)
    for z in range(1, zs):
        project(core, yi, lax.rem(zi + z, zs))
    take_line(own_rows, str_send, str_line, yi, 0)
    for z in range(zs):
        project(1 - core, yi, z)
    take_y(own_rows, str_send, str_recv)
    push_line(own_rows, str_send, str_line, 1 - yi, 1)
    for z in range(zs):
        project(core, 1 - yi, z)
    take_line(own_rows, str_send, str_line, 1 - yi, 1)
    for z in range(zs):
        project(1 - core, 1 - yi, z)
    inverse = lax.rsqrt(jnp.sum(squares[0], axis=1, keepdims=True) / D + 1e-05)
    projected = (acc2[...] * inverse).astype(BF16)

    outgoing = jnp.dot(chosen_ref[...], projected, preferred_element_type=F32)
    for e in range(n):
        send_buf[e] = outgoing[e * OWN_G * CAP:(e + 1) * OWN_G * CAP, :].astype(BF16)
    for off in range(1, n):
        target = lax.rem(me + off, n)
        copy = pltpu.make_async_remote_copy(
            src_ref=send_buf.at[target], dst_ref=recv_buf.at[me],
            send_sem=a2a_send.at[off], recv_sem=a2a_recv.at[me],
            device_id={"wide": target}, device_id_type=MESH,
        )
        launch(copy)
    out_ref[me] = send_buf[me]
    for off in range(1, n):
        source = lax.rem(me + n - off, n)
        pltpu.make_async_remote_copy(
            src_ref=send_buf.at[source], dst_ref=recv_buf.at[source],
            send_sem=a2a_send.at[off], recv_sem=a2a_recv.at[source],
            device_id={"wide": source}, device_id_type=MESH,
        ).wait_recv()
        out_ref[source] = recv_buf[source]
    for wait in started:
        wait()


def body(
    queries, prefix_kv, suffix_kv, counts, residual, out_weight, norm_gain, qkv_weight, owners
):
    n = lax.axis_size("wide")
    zs = n // 4
    cols1 = out_weight.shape[1]
    cols2 = qkv_weight.shape[1]
    half_cols = HALF_GROUPS * HD
    live = n * LIVE
    vmem = pl.BlockSpec(memory_space=pltpu.VMEM)
    smem = pl.BlockSpec(memory_space=pltpu.SMEM)
    anywhere = pl.BlockSpec(memory_space=pl.ANY)
    dma = pltpu.SemaphoreType.DMA
    received = pl.pallas_call(
        functools.partial(kernel, n),
        out_shape=jax.ShapeDtypeStruct((n, OWN_G * CAP, cols2), BF16),
        in_specs=[anywhere] * 3 + [smem] + [anywhere] * 4 + [smem],
        out_specs=vmem,
        scratch_shapes=[
            pltpu.VMEM((KVH, CAP * GQ, HD), F32),
            pltpu.VMEM((PAD * GQ, HD), F32),
            pltpu.VMEM((2, 2, CTX, half_cols), BF16),
            pltpu.VMEM((2, CAP, 2, SUF, half_cols), BF16),
            pltpu.VMEM((D, cols1), BF16),
            pltpu.VMEM((D, cols2), BF16),
            pltpu.VMEM((HALF_GROUPS, PAD, GROUP_COLS), BF16),
            pltpu.VMEM((2, HALF_GROUPS, PAD, GROUP_COLS), BF16),
            pltpu.VMEM((2, 2, zs, 2 * CAP, HALF), BF16),
            pltpu.VMEM((n * CAP, cols1), F32),
            pltpu.VMEM((2, 2, zs, live, cols1), BF16),
            pltpu.VMEM((live, cols2), F32),
            pltpu.VMEM((n, OWN_G * CAP, cols2), BF16),
            pltpu.VMEM((n, OWN_G * CAP, cols2), BF16),
            pltpu.VMEM(queries.shape, BF16),
            pltpu.VMEM(residual.shape, BF16),
            pltpu.VMEM((1, D), F32),
            pltpu.VMEM((live, n * CAP), BF16),
            pltpu.VMEM((n * OWN_G * CAP, live), BF16),
            dma((9,)),
            dma((2,)),
            dma((4 * zs + 1,)),
            dma((2, zs)),
            dma((2,)),
            dma((4 * zs + 1,)),
            dma((2, zs)),
            dma((2,)),
            dma((n,)),
            dma((n,)),
        ],
        compiler_params=pltpu.CompilerParams(
            collective_id=0, has_side_effects=True, vmem_limit_bytes=60 * 1024 * 1024
        ),
    )(
        queries, prefix_kv, suffix_kv, counts, residual, out_weight, norm_gain[None, :],
        qkv_weight, owners.T,
    )
    received = received.reshape(KVH, n // KVH, OWN_G * CAP, cols2)
    return received.transpose(2, 0, 1, 3).reshape(1, OWN_G, CAP, KVH, GCOLS)


def solution(mesh):
    placed = (
        P(("groups", "wide"), None, None),
        P(("groups", "wide"), None, None, None),
        P(("groups", "wide"), None, None, None, None),
        P("groups"),
        P("groups", "wide"),
        P(None, "wide"),
        P(),
        P(None, "wide"),
        P(),
    )
    return jax.shard_map(
        body,
        mesh=mesh,
        in_specs=placed,
        out_specs=P(("groups", "wide"), None, None, None, None),
        check_vma=False,
    )
```

```python
import functools

import jax
import jax.numpy as jnp
from jax import lax
from jax.experimental import pallas as pl
from jax.experimental.pallas import tpu as pltpu
from jax.sharding import PartitionSpec as P

KVH = 8
HD = 128
D = 8192
GQ = 8
GCOLS = 1280
CTX = 1024
SUF = 64
CAP = 12
OWN_G = 2
LIVE = 8
PAD = 16
GROUP_COLS = GQ * HD
HALF = D // 2
HALF_GROUPS = KVH // 2
KC = 512
ATT_PIECES = 2
PIECE_GROUPS = HALF_GROUPS // ATT_PIECES
PIECE_COLS = PIECE_GROUPS * GROUP_COLS
MESH = pl.DeviceIdType.MESH
BF16 = jnp.bfloat16
F32 = jnp.float32


def kernel(
    n,
    q_hbm, prefix_hbm, suffix_hbm, counts_ref, residual_hbm, w1_hbm, gain_hbm, w2_hbm, owners_ref,
    out_ref,
    qs, mixed_rows, prefix, suffix, w1, w2, swap_out, swap_in, att, acc1, own_rows, acc2, send_buf,
    recv_buf,
    q_ref, residual_ref, gain_ref, compact_ref, chosen_ref,
    load_sem, swap_sem, att_send, att_recv, att_line, str_send, str_recv, str_line, a2a_send,
    a2a_recv,
):
    zs = n // 4
    me = lax.axis_index("wide")
    core = lax.rem(me, 2)
    chip = me // 2
    yi = lax.rem(chip, 2)
    zi = chip // 2
    sib = me + 1 - 2 * core
    live = n * LIVE
    cols1 = w1.shape[1]
    half_cols = HALF_GROUPS * HD

    load_q = pltpu.make_async_copy(q_hbm, q_ref, load_sem.at[6])
    load_q.start()
    halves = (1 - core, core)
    loads = []
    for i, half in enumerate(halves):
        cols = pl.ds(pl.multiple_of(half * half_cols, half_cols), half_cols)
        a = pltpu.make_async_copy(
            prefix_hbm.at[0, :, :, cols], prefix.at[i], load_sem.at[2 * i]
        )
        b = pltpu.make_async_copy(
            suffix_hbm.at[0, :, :, :, cols], suffix.at[i], load_sem.at[2 * i + 1]
        )
        a.start()
        b.start()
        loads.append((a, b))
    load_residual = pltpu.make_async_copy(residual_hbm, residual_ref, load_sem.at[7])
    load_gain = pltpu.make_async_copy(gain_hbm, gain_ref, load_sem.at[8])
    load_residual.start()
    load_gain.start()
    load_w1 = pltpu.make_async_copy(w1_hbm, w1, load_sem.at[4])
    load_w2 = pltpu.make_async_copy(w2_hbm, w2, load_sem.at[5])

    barrier = pltpu.get_barrier_semaphore()
    for off in range(1, n):
        pl.semaphore_signal(
            barrier, inc=1, device_id={"wide": lax.rem(me + off, n)}, device_id_type=MESH
        )

    other_y = (zi * 2 + 1 - yi) * 2 + core
    above, below = me + 4, me - 4
    has_above, has_below = zi < zs - 1, zi > 0
    started = []

    def copy_of(block, send, recv, device):
        return pltpu.make_async_remote_copy(
            src_ref=block, dst_ref=block, send_sem=send, recv_sem=recv,
            device_id={"wide": device}, device_id_type=MESH,
        )

    def launch(copy):
        copy.start()
        started.append(copy.wait_send)

    def launch_if(condition, make):
        pl.when(condition)(lambda: make().start())
        started.append(lambda: pl.when(condition)(lambda: make().wait_send()))

    def push_own(buf, sends, recvs):
        block, recv = buf.at[core, yi, zi], recvs.at[yi, zi]
        launch_if(has_above, lambda: copy_of(block, sends.at[0], recv, above))
        launch_if(has_below, lambda: copy_of(block, sends.at[1], recv, below))
        launch(copy_of(block, sends.at[2], recv, other_y))

    def line_steps(visit):
        for step in range(1, zs):
            visit(2 * step - 2, zi - step, zi >= step, has_above, above)
            visit(2 * step - 1, zi + step, zi + step < zs, has_below, below)

    def pass_z(buf, sends, recvs):
        def visit(index, z, there, onward, device):
            def copy(which, target):
                return copy_of(
                    buf.at[core, yi, z], sends.at[which], recvs.at[yi, z], target
                )

            pl.when(there)(lambda: copy(0, other_y).wait_recv())
            launch_if(there & onward, lambda: copy(3 + 2 * index, device))
            launch_if(there, lambda: copy(4 + 2 * index, other_y))

        line_steps(visit)

    def take_y(buf, sends, recvs):
        def take(z):
            copy_of(
                buf.at[core, 1 - yi, z], sends.at[0], recvs.at[1 - yi, z], other_y
            ).wait_recv()

        take(zi)
        line_steps(lambda index, z, there, onward, device: pl.when(there)(lambda: take(z)))

    def push_line(buf, sends, recvs, y, which):
        launch(copy_of(buf.at[core, y], sends.at[4 * zs - 1 + which], recvs.at[which], sib))

    def take_line(buf, sends, recvs, y, which):
        copy_of(buf.at[1 - core, y], sends.at[0], recvs.at[which], sib).wait_recv()

    load_q.wait()
    for g in range(KVH):
        for q in range(GQ):
            col = (g * GQ + q) * HD
            qs[g, pl.ds(q, CAP, stride=GQ), :] = q_ref[0, :, col:col + HD].astype(F32)
    mixed_rows[...] = jnp.zeros_like(mixed_rows)
    live_count = counts_ref[me]
    slot_valid = lax.broadcasted_iota(jnp.int32, (PAD, HD), 0) < live_count
    rows = CAP * GQ
    suf_cols = CAP * SUF
    suf_mask = (
        lax.broadcasted_iota(jnp.int32, (rows, suf_cols), 0) // GQ
        == lax.broadcasted_iota(jnp.int32, (rows, suf_cols), 1) // SUF
    )
    scale = HD ** (-0.5) * 1.4426950408889634
    nt = (((1,), (1,)), ((), ()))

    def attend(i, half, gg, target):
        query = qs[half * HALF_GROUPS + gg].astype(BF16)
        cols = slice(gg * HD, (gg + 1) * HD)
        keys = prefix[i, 0, :, cols]
        values = prefix[i, 1, :, cols]
        near_keys = suffix[i, :, 0, :, cols].reshape(suf_cols, HD)
        near_values = suffix[i, :, 1, :, cols].reshape(suf_cols, HD)
        far = lax.dot_general(query, keys, nt, preferred_element_type=F32)
        every = lax.dot_general(query, near_keys, nt, preferred_element_type=F32)
        near = jnp.concatenate(
            [every[r * GQ:(r + 1) * GQ, r * SUF:(r + 1) * SUF] for r in range(CAP)], axis=0
        )
        top = jnp.maximum(
            jnp.max(far, axis=1, keepdims=True), jnp.max(near, axis=1, keepdims=True)
        )
        far = jnp.exp2((far - top) * scale)
        near = jnp.exp2((near - top) * scale)
        total = jnp.sum(far, axis=1, keepdims=True) + jnp.sum(near, axis=1, keepdims=True)
        mixed = jnp.dot(far.astype(BF16), values, preferred_element_type=F32)
        spread = jnp.where(suf_mask, jnp.concatenate([near] * CAP, axis=1), 0.0).astype(BF16)
        mixed = mixed + jnp.dot(spread, near_values, preferred_element_type=F32)
        mixed_rows[0:rows, :] = mixed / total
        for q in range(GQ):
            part = jnp.where(slot_valid, mixed_rows[pl.ds(q, PAD, stride=GQ), :], 0.0)
            target[:, q * HD:(q + 1) * HD] = part.astype(BF16)

    pair_i = lax.broadcasted_iota(jnp.int32, (2 * CAP, 2 * PAD), 0)
    pair_j = lax.broadcasted_iota(jnp.int32, (2 * CAP, 2 * PAD), 1)
    from_core = pair_i // CAP
    wanted = jnp.where(from_core == core, 0, PAD) + lax.rem(pair_i, CAP)
    pick = (wanted == pair_j).astype(F32).astype(BF16)

    def att_refs(piece):
        return att.at[piece], att_send.at[piece], att_recv.at[piece]

    def att_lines(piece):
        return att.at[piece], att_send.at[piece], att_line.at[piece]

    for piece in range(ATT_PIECES):
        groups = range(piece * PIECE_GROUPS, (piece + 1) * PIECE_GROUPS)
        if piece == 0:
            loads[0][0].wait()
            loads[0][1].wait()
        for gg in groups:
            attend(0, halves[0], gg, swap_out.at[gg])
        if piece == 0:
            pl.semaphore_wait(barrier, n - 1)
        part = pl.ds(piece * PIECE_GROUPS, PIECE_GROUPS)
        swap = pltpu.make_async_remote_copy(
            src_ref=swap_out.at[part], dst_ref=swap_in.at[1, part],
            send_sem=swap_sem.at[0, piece], recv_sem=swap_sem.at[1, piece],
            device_id={"wide": sib}, device_id_type=MESH,
        )
        launch(swap)
        if piece == 0:
            loads[1][0].wait()
            loads[1][1].wait()
            load_w1.start()
            load_w2.start()
        for gg in groups:
            attend(1, halves[1], gg, swap_in.at[0, gg])
        swap.wait_recv()
        for gg in groups:
            both = jnp.concatenate([swap_in[0, gg], swap_in[1, gg]], axis=0)
            col = gg % PIECE_GROUPS * GROUP_COLS
            att[piece, core, yi, zi, :, col:col + GROUP_COLS] = jnp.dot(
                pick, both, preferred_element_type=F32
            ).astype(BF16)
        push_own(*att_refs(piece))

    column = lax.broadcasted_iota(jnp.int32, (1, n * CAP), 1)
    place_chip = column // (2 * CAP)
    place_chip = lax.rem(place_chip, zs) * 2 + place_chip // zs
    parent = place_chip * 2 + lax.rem(column // CAP, 2)
    slot = lax.rem(column, CAP)
    place = jnp.full((1, n * CAP), -1, jnp.int32)
    offset = jnp.int32(0)
    for p in range(n):
        count = counts_ref[p]
        place = jnp.where((parent == p) & (slot < count), slot + offset, place)
        offset = offset + count
    compact = lax.broadcasted_iota(jnp.int32, (live, n * CAP), 0) == place
    compact_ref[...] = compact.astype(F32).astype(BF16)

    load_residual.wait()
    load_gain.wait()
    residual = residual_ref[...].astype(F32)
    for y in range(2):
        for z in range(zs):
            to, source = (y * zs + z) * 2 * CAP, (z * 2 + y) * 2 * CAP
            acc1[to:to + 2 * CAP, :] = residual[source:source + 2 * CAP, :]

    def out_project(piece, half, y):
        line_rows = zs * 2 * CAP
        place = pl.ds(pl.multiple_of(y * line_rows, line_rows), line_rows)

        @pl.loop(0, PIECE_COLS // KC)
        def _(step):
            col = pl.multiple_of(step * KC, KC)
            block = att[piece, half, y, :, :, pl.ds(col, KC)].astype(F32)
            block = block.reshape(line_rows, KC).astype(BF16)
            row = pl.multiple_of(half * HALF + piece * PIECE_COLS + col, KC)
            acc1[place, :] += jnp.dot(block, w1[pl.ds(row, KC), :], preferred_element_type=F32)

    for piece in range(ATT_PIECES):
        pass_z(*att_refs(piece))
        push_line(*att_lines(piece), yi, 0)
    load_w1.wait()
    out_project(0, core, yi)
    for piece in range(ATT_PIECES):
        take_line(*att_lines(piece), yi, 0)
        out_project(piece, 1 - core, yi)
        take_y(*att_refs(piece))
        push_line(*att_lines(piece), 1 - yi, 1)
        if piece + 1 < ATT_PIECES:
            out_project(piece + 1, core, yi)
        out_project(piece, core, 1 - yi)
        take_line(*att_lines(piece), 1 - yi, 1)
        out_project(piece, 1 - core, 1 - yi)

    stream = acc1[...].astype(BF16)
    own_rows[core, yi, zi] = jnp.dot(
        compact_ref[...], stream, preferred_element_type=F32
    ).astype(BF16)
    push_own(own_rows, str_send, str_recv)

    kv_group = me // (n // KVH)
    lines = n * OWN_G * CAP
    line = lax.broadcasted_iota(jnp.int32, (1, lines), 1)
    line_owner = line // (OWN_G * CAP)
    line_rank = lax.rem(line // CAP, OWN_G)
    line_slot = lax.rem(line, CAP)
    seen = jnp.zeros((1, lines), jnp.int32)
    place = jnp.full((1, lines), -1, jnp.int32)
    offset = jnp.int32(0)
    for p in range(n):
        count = counts_ref[p]
        member = line_owner == owners_ref[kv_group, p]
        hit = member & (seen == line_rank) & (line_slot < count)
        place = jnp.where(hit, line_slot + offset, place)
        seen = seen + member.astype(jnp.int32)
        offset = offset + count
    chosen = (lax.broadcasted_iota(jnp.int32, (live, lines), 0) == place).astype(F32)
    chosen_ref[...] = chosen.T.astype(BF16)

    load_w2.wait()
    acc2[...] = jnp.zeros_like(acc2)
    squares = [jnp.zeros((live, 128), F32)]

    def project(half, y, z):
        base = ((z * 2 + y) * 2 + half) * cols1
        cols = pl.ds(pl.multiple_of(base, cols1), cols1)
        block = own_rows[half, y, z].astype(F32)
        for k in range(cols1 // 128):
            part = block[:, k * 128:(k + 1) * 128]
            squares[0] = squares[0] + part * part
        scaled = (block * gain_ref[0:1, cols]).astype(BF16)
        acc2[...] += jnp.dot(scaled, w2[cols, :], preferred_element_type=F32)

    project(core, yi, zi)
    pass_z(own_rows, str_send, str_recv)
    push_line(own_rows, str_send, str_line, yi, 0)
    for z in range(1, zs):
        project(core, yi, lax.rem(zi + z, zs))
    take_line(own_rows, str_send, str_line, yi, 0)
    for z in range(zs):
        project(1 - core, yi, z)
    take_y(own_rows, str_send, str_recv)
    push_line(own_rows, str_send, str_line, 1 - yi, 1)
    for z in range(zs):
        project(core, 1 - yi, z)
    take_line(own_rows, str_send, str_line, 1 - yi, 1)
    for z in range(zs):
        project(1 - core, 1 - yi, z)
    inverse = lax.rsqrt(jnp.sum(squares[0], axis=1, keepdims=True) / D + 1e-05)
    projected = (acc2[...] * inverse).astype(BF16)

    outgoing = jnp.dot(chosen_ref[...], projected, preferred_element_type=F32)
    for e in range(n):
        send_buf[e] = outgoing[e * OWN_G * CAP:(e + 1) * OWN_G * CAP, :].astype(BF16)
    for off in range(1, n):
        target = lax.rem(me + off, n)
        copy = pltpu.make_async_remote_copy(
            src_ref=send_buf.at[target], dst_ref=recv_buf.at[me],
            send_sem=a2a_send.at[off], recv_sem=a2a_recv.at[me],
            device_id={"wide": target}, device_id_type=MESH,
        )
        launch(copy)
    out_ref[me] = send_buf[me]
    for off in range(1, n):
        source = lax.rem(me + n - off, n)
        pltpu.make_async_remote_copy(
            src_ref=send_buf.at[source], dst_ref=recv_buf.at[source],
            send_sem=a2a_send.at[off], recv_sem=a2a_recv.at[source],
            device_id={"wide": source}, device_id_type=MESH,
        ).wait_recv()
        out_ref[source] = recv_buf[source]
    for wait in started:
        wait()


def body(
    queries, prefix_kv, suffix_kv, counts, residual, out_weight, norm_gain, qkv_weight, owners
):
    n = lax.axis_size("wide")
    zs = n // 4
    cols1 = out_weight.shape[1]
    cols2 = qkv_weight.shape[1]
    half_cols = HALF_GROUPS * HD
    live = n * LIVE
    vmem = pl.BlockSpec(memory_space=pltpu.VMEM)
    smem = pl.BlockSpec(memory_space=pltpu.SMEM)
    anywhere = pl.BlockSpec(memory_space=pl.ANY)
    dma = pltpu.SemaphoreType.DMA
    received = pl.pallas_call(
        functools.partial(kernel, n),
        out_shape=jax.ShapeDtypeStruct((n, OWN_G * CAP, cols2), BF16),
        in_specs=[anywhere] * 3 + [smem] + [anywhere] * 4 + [smem],
        out_specs=vmem,
        scratch_shapes=[
            pltpu.VMEM((KVH, CAP * GQ, HD), F32),
            pltpu.VMEM((PAD * GQ, HD), F32),
            pltpu.VMEM((2, 2, CTX, half_cols), BF16),
            pltpu.VMEM((2, CAP, 2, SUF, half_cols), BF16),
            pltpu.VMEM((D, cols1), BF16),
            pltpu.VMEM((D, cols2), BF16),
            pltpu.VMEM((HALF_GROUPS, PAD, GROUP_COLS), BF16),
            pltpu.VMEM((2, HALF_GROUPS, PAD, GROUP_COLS), BF16),
            pltpu.VMEM((ATT_PIECES, 2, 2, zs, 2 * CAP, PIECE_COLS), BF16),
            pltpu.VMEM((n * CAP, cols1), F32),
            pltpu.VMEM((2, 2, zs, live, cols1), BF16),
            pltpu.VMEM((live, cols2), F32),
            pltpu.VMEM((n, OWN_G * CAP, cols2), BF16),
            pltpu.VMEM((n, OWN_G * CAP, cols2), BF16),
            pltpu.VMEM(queries.shape, BF16),
            pltpu.VMEM(residual.shape, BF16),
            pltpu.VMEM((1, D), F32),
            pltpu.VMEM((live, n * CAP), BF16),
            pltpu.VMEM((n * OWN_G * CAP, live), BF16),
            dma((9,)),
            dma((2, ATT_PIECES)),
            dma((ATT_PIECES, 4 * zs + 1)),
            dma((ATT_PIECES, 2, zs)),
            dma((ATT_PIECES, 2)),
            dma((4 * zs + 1,)),
            dma((2, zs)),
            dma((2,)),
            dma((n,)),
            dma((n,)),
        ],
        compiler_params=pltpu.CompilerParams(
            collective_id=0, has_side_effects=True, vmem_limit_bytes=60 * 1024 * 1024
        ),
    )(
        queries, prefix_kv, suffix_kv, counts, residual, out_weight, norm_gain[None, :],
        qkv_weight, owners.T,
    )
    received = received.reshape(KVH, n // KVH, OWN_G * CAP, cols2)
    return received.transpose(2, 0, 1, 3).reshape(1, OWN_G, CAP, KVH, GCOLS)


def solution(mesh):
    placed = (
        P(("groups", "wide"), None, None),
        P(("groups", "wide"), None, None, None),
        P(("groups", "wide"), None, None, None, None),
        P("groups"),
        P("groups", "wide"),
        P(None, "wide"),
        P(),
        P(None, "wide"),
        P(),
    )
    return jax.shard_map(
        body,
        mesh=mesh,
        in_specs=placed,
        out_specs=P(("groups", "wide"), None, None, None, None),
        check_vma=False,
    )
```
